256 devices in a mesh: dcn: 2 (over x_lo), dp: 16 (over x_hi, y, core), tp: 8 (over z).
Axes of the slice: x: 4 (x_hi: 2, x_lo: 2; x = x_hi * 2 + x_lo), y: 4, z: 8, core: 2. Of those that a mesh axis runs over, the one named last changes fastest.
Arguments:
- tokens: bfloat16 [4096, 18432], P(('dcn', 'dp', 'tp')), may hold values from -24 to 24
- upstream: bfloat16 [4096, 18432], P(('dcn', 'dp', 'tp')), may hold values from -5 to 5
- w_in: bfloat16 [18432, 1024], P(None, 'tp'), may hold values from -0.046875 to 0.046875
- w_out: bfloat16 [1024, 18432], P('tp'), may hold values from -0.1875 to 0.1875
Outputs:
- tokens_grad: float32 [4096, 18432], P(('dcn', 'dp', 'tp'))
- in_grad: float32 [18432, 1024], P(('dcn', 'dp'), 'tp')
- out_grad: float32 [1024, 18432], P('tp', ('dcn', 'dp'))
The draws below stay inside these ranges and needn't reach their ends.
All inputs are finite; a program needn't handle non-finite values.
Results may differ from the reference program's by a relative error of at most 0.0029.
Values may be sent and summed in bfloat16 or wider, within the bound.
A program may use at most 128 MiB of HBM per device.

```python
import jax
import jax.numpy as jnp

D = 18432
TOK_DEV = 16
HID = 1024
TOKENS = 4096
N_TP = 8


def raised(array, rng, source, target, blocks, factor):
    owner, partner = [(jnp.arange(array.shape[axis_at]) // (array.shape[axis_at] // blocks)).reshape([-1 if axis == axis_at else 1 for axis in range(array.ndim)]) for axis_at in (source, target)]
    chosen = jax.random.permutation(rng, blocks)[partner]
    strong = (owner == chosen) | (owner == (partner + blocks // 2) % blocks)
    return jnp.where(strong, factor * array, array)


def level_of(key, dims, shards, smallest, high):
    def one(axis_at, blocks):
        heights = jax.random.uniform(jax.random.fold_in(jax.random.fold_in(key, 6), axis_at), (blocks,), jnp.float32, smallest / len(shards), high / len(shards))
        return jnp.repeat(jnp.exp(heights), dims[axis_at] // blocks).reshape((-1,) + (1,) * (len(dims) - axis_at - 1))

    factor_of = one(*shards[0])
    for cut in shards[1:]:
        factor_of = factor_of * one(*cut)
    return factor_of


def centred(key, dims, width, bound, split=(), kind=jnp.bfloat16):
    loudness = level_of(key, dims, split, -0.22, 0.18) if split else 1.0
    values = jax.random.normal(key, dims, jnp.float32) * width * loudness
    return jnp.minimum(jnp.maximum(values, -bound), bound).astype(kind)


def noise_with(rng, dims, scale, reach, pieces, heavy, dtype=jnp.bfloat16):
    entries = scale * jax.random.normal(rng, dims, jnp.float32)
    if pieces:
        entries = entries * level_of(rng, dims, pieces, -0.22, 0.18)
    return jnp.clip(raised(entries, jax.random.fold_in(rng, 3), *heavy), -reach, reach).astype(dtype)


def setup_inputs(seed: int = 0) -> dict:
    seeds = jax.random.split(jax.random.key(seed), 5)
    return {
        "tokens": noise_with(seeds[0], (TOKENS, D), 1.0, 24.0, ((0, 256),), (0, 1, 256, 6.0)),
        "upstream": noise_with(seeds[1], (TOKENS, D), ((TOK_DEV * N_TP) ** -0.5), 5.0, ((0, 256),), (0, 1, 256, 6.0)),
        "w_in": centred(seeds[2], (D, HID), D ** -0.5, 0.046875, ((1, 8),)),
        "w_out": centred(seeds[3], (HID, D), HID ** -0.5, 0.1875, ((0, 8),)),
    }


def reference(tokens, upstream, w_in, w_out):
    pre = jnp.dot(tokens, w_in, preferred_element_type=jnp.float32)
    positive = jnp.maximum(pre, 0.0)
    act = (positive * positive).astype(jnp.bfloat16)
    out_grad = jnp.dot(act.T, upstream, preferred_element_type=jnp.float32)
    act_grad = jnp.dot(upstream, w_out.T, preferred_element_type=jnp.float32)
    pre_grad = (act_grad * 2.0 * positive).astype(jnp.bfloat16)
    in_grad = jnp.dot(tokens.T, pre_grad, preferred_element_type=jnp.float32)
    tokens_grad = jnp.dot(pre_grad, w_in.T, preferred_element_type=jnp.float32)
    return tokens_grad, in_grad, out_grad
```

```python
import functools

import jax
import jax.numpy as jnp
from jax import lax
from jax.experimental import pallas as pl
from jax.experimental.pallas import tpu as pltpu
from jax.sharding import PartitionSpec as P

MESH = pl.DeviceIdType.MESH
F32 = jnp.float32
BF16 = jnp.bfloat16


def mult(value, of):
    return pl.multiple_of(value, of)


def kernel(
    cfg,
    tokens, upstream, w_in, w_out,
    tg_out, ing_out, outg_out,
    tokb, upb, tokT, upT, w1, w2, wo_tmp,
    prep, sibr, urecv, usum, vrecv, pos, gath,
    grad, zsend, zrecv, tgb, tgr, tga, res,
    loc_sem, a2a_send, a2a_recv, ag_send, ag_recv, rs_send, rs_recv,
    sib_send, sib_recv, u_send, u_recv, v_send, v_recv,
):
    NXL, NDP, NZ, NS, T, B, W, HID = cfg
    NP = NXL * NDP
    H = NZ // 2
    R = NP * T
    HR = R // 2
    HB = B // 2
    TS = min(256, HID)
    NT = HID // TS

    z = lax.axis_index("tp")
    dcn = lax.axis_index("dcn")
    dp = lax.axis_index("dp")
    k = dp % 2
    y = (dp // 2) % NS
    x = (dp // (2 * NS)) * NXL + dcn
    me = dcn * NDP + dp
    u = jnp.where(k == 0, x, y)
    v = jnp.where(k == 0, y, x)

    def dev(x_, y_, k_):
        return (x_ % NXL, (x_ // NXL) * (2 * NS) + y_ * 2 + k_, z)

    def dev_i(i_):
        return (i_ // NDP, i_ % NDP, z)

    sib = dev(x, y, 1 - k)

    def u_peer(u_):
        return dev(jnp.where(k == 0, u_, x), jnp.where(k == 0, y, u_), k)

    def v_peer(v_):
        return dev(jnp.where(k == 0, x, v_), jnp.where(k == 0, v_, y), k)

    right = (dcn, dp, (z + 1) % NZ)
    left = (dcn, dp, (z + NZ - 1) % NZ)
    zn = (right, left)

    def lane0(i_):
        return mult(128 * ((B // 64) * (i_ // 2) + (B // 128) * (i_ % 2)), 128)

    row0 = mult(64 * k, 64)
    pad0 = mult(jnp.where(k == 0, B, 0), 64)
    sends = []

    def send(src, dst, ss, rs, to):
        c = pltpu.make_async_remote_copy(
            src_ref=src, dst_ref=dst, send_sem=ss, recv_sem=rs, device_id=to, device_id_type=MESH
        )
        c.start()
        sends.append(c)
        return c

    barrier = pltpu.get_barrier_semaphore()

    @pl.loop(1, NP)
    def _(d):
        pl.semaphore_signal(barrier, inc=1, device_id=dev_i((me + d) % NP), device_id_type=MESH)

    pl.semaphore_signal(barrier, inc=1, device_id=right, device_id_type=MESH)
    if NZ > 2:
        pl.semaphore_signal(barrier, inc=1, device_id=left, device_id_type=MESH)

    my_lane = lane0(me)
    own = pl.ds(mult(128 * z, 128), 128)
    c_win = pltpu.make_async_copy(
        w_in.at[pl.ds(mult(B * me, 64), B), :], w1.at[pl.ds(row0, B), own], loc_sem.at[0]
    )
    c_win.start()
    c_wout = pltpu.make_async_copy(w_out.at[:, pl.ds(my_lane, W)], wo_tmp, loc_sem.at[1])
    c_wout.start()
    my_rows = pl.ds(mult(T * me, T), T)
    c_tok = pltpu.make_async_copy(tokens.at[:, pl.ds(my_lane, W)], tokb.at[my_rows, :], loc_sem.at[2])
    c_tok.start()
    c_up = pltpu.make_async_copy(upstream.at[:, pl.ds(my_lane, W)], upb.at[my_rows, :], loc_sem.at[3])
    c_up.start()
    w1[pl.ds(pad0, 64), :] = jnp.zeros((64, HID), BF16)
    w2[pl.ds(pad0, 64), :] = jnp.zeros((64, HID), BF16)
    c_wout.wait()
    w2[pl.ds(row0, B), own] = jnp.where(
        k == 0, wo_tmp[:, 0:B].T, wo_tmp[:, W - B : W].T
    )
    c_win.wait()
    pl.semaphore_wait(barrier, NP + (1 if NZ > 2 else 0))

    def part(hf):
        return pl.ds(mult(row0 + HB * hf, 16), HB)

    def halves(step, d):
        return (0, 1) if step < H - 1 else (d,)

    def ag_block(w, wi, step, d, hf, start):
        if start:
            blk = (z + NZ - step) % NZ if d == 0 else (z + step) % NZ
        else:
            blk = (z + NZ - 1 - step) % NZ if d == 0 else (z + 1 + step) % NZ
        ref = w.at[part(hf), pl.ds(mult(128 * blk, 128), 128)]
        n = ((wi * 2 + d) * H + step) * 2 + hf
        return ref, ag_send.at[n], ag_recv.at[n]

    def ag_start(w, wi, step):
        for hf in (0, 1):
            for d in (0, 1):
                if hf in halves(step, d):
                    ref, ss, rs = ag_block(w, wi, step, d, hf, True)
                    send(ref, ref, ss, rs, zn[d])

    def ag_wait(w, wi, step, hf, d):
        ref, ss, rs = ag_block(w, wi, step, d, hf, False)
        pltpu.make_async_copy(ref, ref, rs).wait()

    def ag_step(w, wi, step):
        for hf in (0, 1):
            for d in (0, 1):
                if hf in halves(step, d):
                    ag_wait(w, wi, step, hf, d)
                    if step + 1 < H and hf in halves(step + 1, d):
                        ref, ss, rs = ag_block(w, wi, step + 1, d, hf, True)
                        send(ref, ref, ss, rs, zn[d])

    def a2a_start(src, dst, n):
        @pl.loop(1, NP)
        def _(dd):
            to = (me + dd) % NP
            pltpu.make_async_remote_copy(
                src_ref=src.at[:, pl.ds(lane0(to), W)],
                dst_ref=dst.at[my_rows, :],
                send_sem=a2a_send.at[n],
                recv_sem=a2a_recv.at[n],
                device_id=dev_i(to),
                device_id_type=MESH,
            ).start()

    def a2a_wait(buf, n, sems):
        ref = buf.at[pl.ds(0, R - T), :]
        pltpu.make_async_copy(ref, ref, sems.at[n]).wait()

    ag_start(w1, 0, 0)
    a2a_start(tokens, tokb, 0)
    if H > 1:
        ag_step(w1, 0, 0)
    a2a_start(upstream, upb, 1)
    for s in range(1 if H > 1 else 0, H):
        ag_step(w1, 0, s)
        if s == max(H - 2, 0):
            ag_start(w2, 1, 0)
    c_tok.wait()
    a2a_wait(tokb, 0, a2a_recv)

    my_half = mult(HR * k, HR)
    sib_half = mult(HR * (1 - k), HR)
    UR = HR // NS

    def mm_half(lhs, w, n, start):
        @pl.loop(0, NT)
        def _(t):
            cols = pl.ds(mult(TS * t, TS), TS)
            prep[n, pl.ds(start, HR), cols] = jnp.dot(
                lhs[pl.ds(start, HR), :], w[:, cols], preferred_element_type=F32
            )

    def presum_start(lhs, w, n):
        mm_half(lhs, w, n, sib_half)
        rows = prep.at[n, pl.ds(sib_half, HR), :]
        c = send(rows, sibr.at[n], sib_send.at[n], sib_recv.at[n], sib)
        mm_half(lhs, w, n, my_half)
        return c

    def presum_end(c, n):
        c.wait_recv()
        out = []
        for r in list(range(1, NS)) + [0]:
            uu = (u + r) % NS
            rows = pl.ds(mult(my_half + UR * uu, UR), UR)
            loc = pl.ds(mult(UR * uu, UR), UR)
            prep[n, rows, :] += sibr[n, loc, :]
            if r:
                out.append(
                    send(prep.at[n, rows, :], urecv.at[n, r - 1], u_send.at[n, r - 1], u_recv.at[n, r - 1], u_peer(uu))
                )
        return out

    def u_end(cs, n):
        rows = pl.ds(mult(my_half + UR * u, UR), UR)
        for c in cs:
            c.wait_recv()
        tot = prep[n, rows, :]
        for r in range(NS - 1):
            tot = tot + urecv[n, r]
        usum[n] = tot
        out = []
        for r in range(1, NS):
            vv = (v + r) % NS
            out.append(
                send(
                    usum.at[n, pl.ds(mult(T * vv, T), T), :], vrecv.at[n, r - 1],
                    v_send.at[n, r - 1], v_recv.at[n, r - 1], v_peer(vv),
                )
            )
        return out

    def v_end(cs, n):
        for c in cs:
            c.wait_recv()
        tot = usum[n, pl.ds(mult(T * v, T), T), :]
        for r in range(NS - 1):
            tot = tot + vrecv[n, r]
        return tot

    def gv_start(n):
        ref = gath.at[n, pl.ds(mult(my_half + UR * u + T * v, T), T), :]
        return [
            send(ref, ref, v_send.at[2 + n, r - 1], v_recv.at[2 + n, r - 1], v_peer((v + r) % NS))
            for r in range(1, NS)
        ]

    def gu_start(cs, n):
        for c in cs:
            c.wait_recv()
        ref = gath.at[n, pl.ds(mult(my_half + UR * u, UR), UR), :]
        return [
            send(ref, ref, u_send.at[2 + n, r - 1], u_recv.at[2 + n, r - 1], u_peer((u + r) % NS))
            for r in range(1, NS)
        ]

    def gs_start(cs, n):
        for c in cs:
            c.wait_recv()
        ref = gath.at[n, pl.ds(my_half, HR), :]
        return send(ref, ref, sib_send.at[2 + n], sib_recv.at[2 + n], sib)

    MT = W // 2

    def grad_mm(lhsT, n):
        @pl.loop(0, NT)
        def _(t):
            cols = pl.ds(mult(TS * t, TS), TS)
            for m in range(2):
                grad[n, pl.ds(MT * m, MT), cols] = jnp.dot(
                    lhsT[pl.ds(MT * m, MT), :], gath[n, :, cols], preferred_element_type=F32
                )

    def grad_block(n, blk, hf):
        return grad[n, part(hf), pl.ds(mult(128 * blk, 128), 128)]

    def rs_idx(n, d, step):
        return (n * 2 + d) * H + step

    def rs_halves(step, d):
        return (d,) if step == 0 else (0, 1)

    def rs_send_block(n, d, step, hf, val):
        q = rs_idx(n, d, step)
        rows = pl.ds(HB * hf, HB)
        zsend[q, rows, :] = val.astype(BF16)
        send(
            zsend.at[q, rows, :], zrecv.at[q, rows, :],
            rs_send.at[q * 2 + hf], rs_recv.at[q * 2 + hf], zn[d],
        )

    def rs_get(n, d, step, hf):
        q = rs_idx(n, d, step)
        rows = pl.ds(HB * hf, HB)
        ref = zrecv.at[q, rows, :]
        pltpu.make_async_copy(ref, ref, rs_recv.at[q * 2 + hf]).wait()
        return zrecv[q, rows, :].astype(F32)

    def rs_dest(d, step):
        return (z + H - step) % NZ if d == 0 else (z + NZ - H + step) % NZ

    def rs_step(n, step):
        order = ((0, 0), (1, 1), (0, 1), (1, 0))
        for d, hf in order:
            if hf in rs_halves(step, d):
                val = grad_block(n, rs_dest(d, step), hf)
                if step >= 1 and hf in rs_halves(step - 1, d):
                    val = val + rs_get(n, d, step - 1, hf)
                rs_send_block(n, d, step, hf, val)

    def rs_end(n):
        for hf in (0, 1):
            val = grad_block(n, z, hf)
            for d in (0, 1):
                if hf in rs_halves(H - 1, d):
                    val = val + rs_get(n, d, H - 1, hf)
            res[n, pl.ds(HB * hf, HB), :] = val

    c = presum_start(tokb, w1, 0)
    if H > 1:
        ag_step(w2, 1, 0)
    cu = presum_end(c, 0)
    for s in range(1, H - 1):
        ag_step(w2, 1, s)
    tokT[...] = tokb[...].T
    cv = u_end(cu, 0)
    ag_step(w2, 1, H - 1)
    c_up.wait()
    a2a_wait(upb, 1, a2a_recv)
    positive = jnp.maximum(v_end(cv, 0), 0.0)
    pos[...] = positive
    gath[0, pl.ds(mult(my_half + UR * u + T * v, T), T), :] = (positive * positive).astype(BF16)
    gv = gv_start(0)
    c = presum_start(upb, w2, 1)
    gu = gu_start(gv, 0)
    cu = presum_end(c, 1)
    gs = gs_start(gu, 0)
    upT[...] = upb[...].T
    gs.wait_recv()
    grad_mm(upT, 0)
    rs_step(0, 0)
    cv = u_end(cu, 1)
    pg = v_end(cv, 1) * 2.0 * pos[...]
    gath[1, pl.ds(mult(my_half + UR * u + T * v, T), T), :] = pg.astype(BF16)
    gv = gv_start(1)
    if H > 1:
        rs_step(0, 1)
    gu = gu_start(gv, 1)
    if H > 2:
        rs_step(0, 2)
    gs = gs_start(gu, 1)
    for s in range(3, H):
        rs_step(0, s)
    gs.wait_recv()
    grad_mm(tokT, 1)
    rs_step(1, 0)

    TR = min(128, R)

    @pl.loop(0, R // TR)
    def _(t):
        rows = pl.ds(mult(TR * t, TR), TR)
        tgb[rows, :] = lax.dot_general(
            gath[1, rows, :], w1[...], (((1,), (1,)), ((), ())), preferred_element_type=F32
        ).astype(BF16)

    @pl.loop(1, NP)
    def _(dd):
        to = (me + dd) % NP
        pltpu.make_async_remote_copy(
            src_ref=tgb.at[pl.ds(mult(T * to, T), T), :],
            dst_ref=tgr.at[my_rows, :],
            send_sem=a2a_send.at[2],
            recv_sem=a2a_recv.at[2],
            device_id=dev_i(to),
            device_id_type=MESH,
        ).start()

    tgr[my_rows, :] = tgb[my_rows, :]
    if H > 1:
        rs_step(1, 1)
    rs_end(0)
    c_o = pltpu.make_async_copy(res.at[0], outg_out, loc_sem.at[0])
    c_o.start()
    if H > 2:
        rs_step(1, 2)
    a2a_wait(tgr, 2, a2a_recv)
    FT = (B // 128) * 128

    @pl.loop(0, NP // 2)
    def _(p):
        base = 2 * B * p
        r0 = pl.ds(mult(2 * T * p, 2 * T), T)
        r1 = pl.ds(mult(2 * T * p + T, T), T)
        tga[:, pl.ds(mult(base, 128), FT)] = tgr[r0, 0:FT]
        tga[:, pl.ds(mult(base + FT, 128), 128)] = tgr[r0, FT:W] + tgr[r1, 0:128]
        tga[:, pl.ds(mult(base + FT + 128, 128), FT)] = tgr[r1, 128:W]

    c_t = pltpu.make_async_copy(tga, tg_out, loc_sem.at[1])
    c_t.start()
    for s in range(3, H):
        rs_step(1, s)
    rs_end(1)
    c_i = pltpu.make_async_copy(res.at[1], ing_out, loc_sem.at[2])
    c_i.start()

    for c in sends:
        c.wait_send()
    a2a_wait(tokb, 0, a2a_send)
    a2a_wait(upb, 1, a2a_send)
    a2a_wait(tgb, 2, a2a_send)
    c_o.wait()
    c_t.wait()
    c_i.wait()


def make(mesh):
    NXL, NDP, NZ = mesh.shape["dcn"], mesh.shape["dp"], mesh.shape["tp"]
    NP = NXL * NDP
    NS = 1
    while NS * NS * 2 < NP:
        NS += 1

    def per_device(tokens, upstream, w_in, w_out):
        T, D = tokens.shape
        B = D // NP
        W = B + 64
        HID = 128 * NZ
        H = NZ // 2
        R = NP * T
        HR = R // 2
        UR = HR // NS
        cfg = (NXL, NDP, NZ, NS, T, B, W, HID)
        DMA = pltpu.SemaphoreType.DMA
        scratch = [
            pltpu.VMEM((R, W), BF16),
            pltpu.VMEM((R, W), BF16),
            pltpu.VMEM((W, R), BF16),
            pltpu.VMEM((W, R), BF16),
            pltpu.VMEM((W, HID), BF16),
            pltpu.VMEM((W, HID), BF16),
            pltpu.VMEM((128, W), BF16),
            pltpu.VMEM((2, R, HID), F32),
            pltpu.VMEM((2, HR, HID), F32),
            pltpu.VMEM((2, NS - 1, UR, HID), F32),
            pltpu.VMEM((2, UR, HID), F32),
            pltpu.VMEM((2, NS - 1, T, HID), F32),
            pltpu.VMEM((T, HID), F32),
            pltpu.VMEM((2, R, HID), BF16),
            pltpu.VMEM((2, W, HID), F32),
            pltpu.VMEM((4 * H, B, 128), BF16),
            pltpu.VMEM((4 * H, B, 128), BF16),
            pltpu.VMEM((R, W), BF16),
            pltpu.VMEM((R, W), BF16),
            pltpu.VMEM((T, D), BF16),
            pltpu.VMEM((2, B, 128), F32),
            DMA((4,)),
            DMA((3,)),
            DMA((3,)),
            DMA((8 * H,)),
            DMA((8 * H,)),
            DMA((8 * H,)),
            DMA((8 * H,)),
            DMA((4,)),
            DMA((4,)),
            DMA((4, NS - 1)),
            DMA((4, NS - 1)),
            DMA((4, NS - 1)),
            DMA((4, NS - 1)),
        ]
        tg, ing, outg = pl.pallas_call(
            functools.partial(kernel, cfg),
            out_shape=(
                jax.ShapeDtypeStruct((T, D), BF16),
                jax.ShapeDtypeStruct((B, 128), F32),
                jax.ShapeDtypeStruct((B, 128), F32),
            ),
            in_specs=[pl.BlockSpec(memory_space=pl.ANY)] * 4,
            out_specs=tuple([pl.BlockSpec(memory_space=pl.ANY)] * 3),
            scratch_shapes=scratch,
            compiler_params=pltpu.CompilerParams(
                collective_id=0, has_side_effects=True, vmem_limit_bytes=56 * 2**20
            ),
        )(tokens, upstream, w_in, w_out)
        return tg.astype(F32), ing, outg.T

    return per_device


def solution(mesh):
    placed = (
        P(("dcn", "dp", "tp"), None),
        P(("dcn", "dp", "tp"), None),
        P(None, "tp"),
        P("tp", None),
    )
    return jax.shard_map(
        make(mesh),
        mesh=mesh,
        in_specs=placed,
        out_specs=(P(("dcn", "dp", "tp"), None), P(("dcn", "dp"), "tp"), P("tp", ("dcn", "dp"))),
        check_vma=False,
    )
```

```python
import functools

import jax
import jax.numpy as jnp
from jax import lax
from jax.experimental import pallas as pl
from jax.experimental.pallas import tpu as pltpu
from jax.sharding import PartitionSpec as P

MESH = pl.DeviceIdType.MESH
F32 = jnp.float32
BF16 = jnp.bfloat16


def mult(value, of):
    return pl.multiple_of(value, of)


def kernel(
    cfg,
    tokens, upstream, w_in, w_out,
    tg_out, ing_out, outg_out,
    tokb, upb, tokT, upT, w1, w2, w1T, wo_tmp,
    prep, sibr, urecv, usum, vrecv, pos, gath,
    grad, zsend, zrecv, tgb, tgr, tga, res,
    loc_sem, a2a_send, a2a_recv, ag_send, ag_recv, rs_send, rs_recv,
    sib_send, sib_recv, u_send, u_recv, v_send, v_recv,
):
    NXL, NDP, NZ, NS, T, B, W, HID = cfg
    NP = NXL * NDP
    H = NZ // 2
    R = NP * T
    HR = R // 2
    HB = B // 2
    TS = min(256, HID)
    NT = HID // TS

    z = lax.axis_index("tp")
    dcn = lax.axis_index("dcn")
    dp = lax.axis_index("dp")
    k = dp % 2
    y = (dp // 2) % NS
    x = (dp // (2 * NS)) * NXL + dcn
    me = dcn * NDP + dp
    u = jnp.where(k == 0, x, y)
    v = jnp.where(k == 0, y, x)

    def dev(x_, y_, k_):
        return (x_ % NXL, (x_ // NXL) * (2 * NS) + y_ * 2 + k_, z)

    def dev_i(i_):
        return (i_ // NDP, i_ % NDP, z)

    sib = dev(x, y, 1 - k)

    def u_peer(u_):
        return dev(jnp.where(k == 0, u_, x), jnp.where(k == 0, y, u_), k)

    def v_peer(v_):
        return dev(jnp.where(k == 0, x, v_), jnp.where(k == 0, v_, y), k)

    right = (dcn, dp, (z + 1) % NZ)
    left = (dcn, dp, (z + NZ - 1) % NZ)
    zn = (right, left)

    def lane0(i_):
        return mult(128 * ((B // 64) * (i_ // 2) + (B // 128) * (i_ % 2)), 128)

    row0 = mult(64 * k, 64)
    pad0 = mult(jnp.where(k == 0, B, 0), 64)
    sends = []

    def send(src, dst, ss, rs, to):
        c = pltpu.make_async_remote_copy(
            src_ref=src, dst_ref=dst, send_sem=ss, recv_sem=rs, device_id=to, device_id_type=MESH
        )
        c.start()
        sends.append(c)
        return c

    def landed(ref, sem):
        pltpu.make_async_copy(ref, ref, sem).wait()

    def drain():
        while sends:
            sends.pop(0).wait_send()

    def slot(m):
        if abs(m) == H:
            return NZ - 1
        return 2 * m if m >= 0 else -2 * m - 1

    def lanes(s):
        return pl.ds(128 * s, 128)

    barrier = pltpu.get_barrier_semaphore()
    my_lane = lane0(me)
    my_rows = pl.ds(mult(T * me, T), T)

    def entry():
        pl.semaphore_signal(barrier, inc=1, device_id=right, device_id_type=MESH)
        if NZ > 2:
            pl.semaphore_signal(barrier, inc=1, device_id=left, device_id_type=MESH)

        @pl.loop(1, NP)
        def _(d):
            pl.semaphore_signal(barrier, inc=1, device_id=dev_i((me + d) % NP), device_id_type=MESH)

    c_win = pltpu.make_async_copy(
        w_in.at[pl.ds(mult(B * me, 64), B), :], w1.at[pl.ds(row0, B), lanes(0)], loc_sem.at[0]
    )
    c_wout = pltpu.make_async_copy(w_out.at[:, pl.ds(my_lane, W)], wo_tmp, loc_sem.at[1])
    c_tok = pltpu.make_async_copy(tokens.at[:, pl.ds(my_lane, W)], tokb.at[my_rows, :], loc_sem.at[2])
    c_up = pltpu.make_async_copy(upstream.at[:, pl.ds(my_lane, W)], upb.at[my_rows, :], loc_sem.at[3])

    def entry_wait():
        c_win.wait()
        pl.semaphore_wait(barrier, NP + (1 if NZ > 2 else 0))

    def own_wout():
        w1[pl.ds(pad0, 64), :] = jnp.zeros((64, HID), BF16)
        w2[pl.ds(pad0, 64), :] = jnp.zeros((64, HID), BF16)
        c_wout.wait()
        w2[pl.ds(row0, B), lanes(0)] = jnp.where(k == 0, wo_tmp[:, 0:B].T, wo_tmp[:, W - B : W].T)

    def part(hf):
        return pl.ds(mult(row0 + HB * hf, 16), HB)

    def halves(step, d):
        return (0, 1) if step < H - 1 else (d,)

    def ag_send_one(wi, step, d, hf):
        w = (w1, w2)[wi]
        sg = 1 if d else -1
        n = ((wi * 2 + d) * H + step) * 2 + hf
        send(
            w.at[part(hf), lanes(slot(sg * step))], w.at[part(hf), lanes(slot(sg * (step + 1)))],
            ag_send.at[n], ag_recv.at[n], zn[d],
        )

    def ag_start(wi):
        for hf in (0, 1):
            for d in (0, 1):
                if hf in halves(0, d):
                    ag_send_one(wi, 0, d, hf)

    def ag(wi, step, hf):
        if step >= H:
            return
        w = (w1, w2)[wi]
        for d in (0, 1):
            if hf in halves(step, d):
                n = ((wi * 2 + d) * H + step) * 2 + hf
                landed(w.at[part(hf), lanes(slot((1 if d else -1) * (step + 1)))], ag_recv.at[n])
                if step + 1 < H and hf in halves(step + 1, d):
                    ag_send_one(wi, step + 1, d, hf)

    def a2a_start(src, dst, n, lo, hi):
        @pl.loop(lo, hi)
        def _(dd):
            to = (me + dd) % NP
            pltpu.make_async_remote_copy(
                src_ref=src.at[:, pl.ds(lane0(to), W)],
                dst_ref=dst.at[my_rows, :],
                send_sem=a2a_send.at[n],
                recv_sem=a2a_recv.at[n],
                device_id=dev_i(to),
                device_id_type=MESH,
            ).start()

    def a2a_wait(buf, n, sems):
        landed(buf.at[pl.ds(0, R - T), :], sems.at[n])

    my_half = mult(HR * k, HR)
    sib_half = mult(HR * (1 - k), HR)
    UR = HR // NS
    mine = pl.ds(mult(my_half + UR * u + T * v, T), T)
    pend = {}

    def chunk(c):
        return pl.ds(TS * c, TS)

    def mm_part(n, c, start):
        lhs, w = ((tokb, w1), (upb, w2))[n]
        prep[n, pl.ds(start, HR), chunk(c)] = jnp.dot(
            lhs[pl.ds(start, HR), :], w[:, chunk(c)], preferred_element_type=F32
        )

    def P_(n, c):
        if c >= NT:
            return
        q = n * NT + c
        mm_part(n, c, sib_half)
        pend["s", n, c] = send(
            prep.at[n, pl.ds(sib_half, HR), chunk(c)], sibr.at[n, :, chunk(c)], sib_send.at[q], sib_recv.at[q], sib
        )
        mm_part(n, c, my_half)

    def S_(n, c):
        if c >= NT:
            return
        q = n * NT + c
        pend["s", n, c].wait_recv()
        out = []
        for r in [2, 1, 3, 0] if NS == 4 else list(range(1, NS)) + [0]:
            uu = (u + r) % NS
            rows = pl.ds(mult(my_half + UR * uu, UR), UR)
            prep[n, rows, chunk(c)] += sibr[n, pl.ds(mult(UR * uu, UR), UR), chunk(c)]
            if r:
                out.append(
                    send(
                        prep.at[n, rows, chunk(c)], urecv.at[n, r - 1, :, chunk(c)],
                        u_send.at[q, r - 1], u_recv.at[q, r - 1], u_peer(uu),
                    )
                )
        pend["u", n, c] = out

    def U_(n, c):
        if c >= NT:
            return
        q = n * NT + c
        for d in pend["u", n, c]:
            d.wait_recv()
        tot = prep[n, pl.ds(mult(my_half + UR * u, UR), UR), chunk(c)]
        for r in range(NS - 1):
            tot = tot + urecv[n, r, :, chunk(c)]
        usum[n, :, chunk(c)] = tot
        pend["v", n, c] = [
            send(
                usum.at[n, pl.ds(mult(T * ((v + r) % NS), T), T), chunk(c)], vrecv.at[n, r - 1, :, chunk(c)],
                v_send.at[q, r - 1], v_recv.at[q, r - 1], v_peer((v + r) % NS),
            )
            for r in range(1, NS)
        ]

    def V_(n, c):
        if c >= NT:
            return
        for d in pend["v", n, c]:
            d.wait_recv()
        tot = usum[n, pl.ds(mult(T * v, T), T), chunk(c)]
        for r in range(NS - 1):
            tot = tot + vrecv[n, r, :, chunk(c)]
        if n == 0:
            positive = jnp.maximum(tot, 0.0)
            pos[:, chunk(c)] = positive
            gath[0, mine, chunk(c)] = (positive * positive).astype(BF16)
        else:
            gath[1, mine, chunk(c)] = (tot * 2.0 * pos[:, chunk(c)]).astype(BF16)
        if (c + 1) % CG == 0:
            GV0(n, c // CG)

    CG = 2 if NT % 2 == 0 else 1
    NG = NT // CG

    def group(g):
        return pl.ds(TS * CG * g, TS * CG)

    def gq(n, g):
        return 2 * NT + n * NG + g

    def GV0(n, g):
        ref = gath.at[n, mine, group(g)]
        pend["gv", n, g] = [
            send(ref, ref, v_send.at[gq(n, g), r - 1], v_recv.at[gq(n, g), r - 1], v_peer((v + r) % NS))
            for r in range(1, NS)
        ]

    def GV(n, g):
        if g >= NG:
            return
        for d in pend["gv", n, g]:
            d.wait_recv()
        ref = gath.at[n, pl.ds(mult(my_half + UR * u, UR), UR), group(g)]
        pend["gu", n, g] = [
            send(ref, ref, u_send.at[gq(n, g), r - 1], u_recv.at[gq(n, g), r - 1], u_peer((u + r) % NS))
            for r in range(1, NS)
        ]

    def GU(n, g):
        if g >= NG:
            return
        for d in pend["gu", n, g]:
            d.wait_recv()
        ref = gath.at[n, pl.ds(my_half, HR), group(g)]
        pend["gs", n, g] = send(ref, ref, sib_send.at[gq(n, g)], sib_recv.at[gq(n, g)], sib)

    def GS(n, g):
        if g >= NG:
            return
        pend["gs", n, g].wait_recv()

    MT = W // 2

    def grad_mm(n, c):
        if c >= NT:
            return
        lhsT = (upT, tokT)[n]

        @pl.loop(0, 2)
        def _(m):
            rows = pl.ds(mult(MT * m, MT), MT)
            grad[n, rows, chunk(c)] = jnp.dot(
                lhsT[rows, :], gath[n, :, chunk(c)], preferred_element_type=F32
            )

    def rs_dest(d, step):
        m = H - step
        return slot(m) if d == 0 else slot(-m)

    def rs_halves(step, d):
        return (d,) if step == 0 else (0, 1)

    def rs_get(n, d, step, hf):
        q = (n * 2 + d) * H + step
        rows = pl.ds(HB * hf, HB)
        landed(zrecv.at[q, rows, :], rs_recv.at[q * 2 + hf])
        return zrecv[q, rows, :].astype(F32)

    def rs_one(n, step, d, hf):
        q = (n * 2 + d) * H + step
        val = grad[n, part(hf), lanes(rs_dest(d, step))]
        if step >= 1 and hf in rs_halves(step - 1, d):
            val = val + rs_get(n, d, step - 1, hf)
        rows = pl.ds(HB * hf, HB)
        zsend[q, rows, :] = val.astype(BF16)
        send(
            zsend.at[q, rows, :], zrecv.at[q, rows, :],
            rs_send.at[q * 2 + hf], rs_recv.at[q * 2 + hf], zn[d],
        )

    def RS(n, step):
        if step >= H:
            return
        if step == 0:
            rs_one(n, 0, 0, 0)
            rs_one(n, 0, 1, 1)
            if H > 1:
                rs_one(n, 1, 0, 1)
                rs_one(n, 1, 1, 0)
        elif step == 1:
            rs_one(n, 1, 0, 0)
            rs_one(n, 1, 1, 1)
        else:
            rs_one(n, step, 0, 1)
            rs_one(n, step, 1, 0)
            rs_one(n, step, 0, 0)
            rs_one(n, step, 1, 1)

    def RS_end(n):
        for hf in (0, 1):
            val = grad[n, part(hf), lanes(0)]
            for d in (0, 1):
                if hf in rs_halves(H - 1, d):
                    val = val + rs_get(n, d, H - 1, hf)
            res[n, pl.ds(HB * hf, HB), :] = val

    def tg_mm(lo, hi):
        @pl.loop(lo * R // 4 // TR, hi * R // 4 // TR)
        def _(t):
            rows = pl.ds(mult(TR * t, TR), TR)
            tgb[rows, :] = jnp.dot(gath[1, rows, :], w1T[...], preferred_element_type=F32).astype(BF16)

    TR = min(128, R // 4)

    def tg_start():
        @pl.loop(1, NP)
        def _(dd):
            to = (me + dd) % NP
            pltpu.make_async_remote_copy(
                src_ref=tgb.at[pl.ds(mult(T * to, T), T), :],
                dst_ref=tgr.at[my_rows, :],
                send_sem=a2a_send.at[2],
                recv_sem=a2a_recv.at[2],
                device_id=dev_i(to),
                device_id_type=MESH,
            ).start()

        tgr[my_rows, :] = tgb[my_rows, :]

    FT = (B // 128) * 128

    def tg_end():
        a2a_wait(tgr, 2, a2a_recv)

        @pl.loop(0, NP // 2)
        def _(p):
            base = 2 * B * p
            r0 = pl.ds(mult(2 * T * p, 2 * T), T)
            r1 = pl.ds(mult(2 * T * p + T, T), T)
            tga[:, pl.ds(mult(base, 128), FT)] = tgr[r0, 0:FT]
            tga[:, pl.ds(mult(base + FT, 128), 128)] = tgr[r0, FT:W] + tgr[r1, 0:128]
            tga[:, pl.ds(mult(base + FT + 128, 128), FT)] = tgr[r1, 128:W]

    def transpose(dst, src):
        dst[...] = src[...].T

    entry()
    for c in (c_win, c_wout, c_tok, c_up):
        c.start()
    entry_wait()
    ag_start(0)
    a2a_start(tokens, tokb, 0, 1, NP)
    own_wout()
    ag(0, 0, 0)
    ag(0, 0, 1)
    a2a_start(upstream, upb, 1, 1, NP // 2)
    ag(0, 1, 0)
    ag(0, 1, 1)
    c_tok.wait()
    a2a_wait(tokb, 0, a2a_recv)
    P_(0, 0)
    ag(0, 2, 0)
    P_(0, 1)
    S_(0, 0)
    ag(0, 2, 1)
    ag_start(1)
    P_(0, 2)
    S_(0, 1)
    ag(0, 3, 0)
    ag(0, 3, 1)
    P_(0, 3)
    S_(0, 2)
    U_(0, 0)
    S_(0, 3)
    a2a_start(upstream, upb, 1, NP // 2, NP)
    ag(1, 0, 0)
    U_(0, 1)
    V_(0, 0)
    ag(1, 0, 1)
    U_(0, 2)
    V_(0, 1)
    U_(0, 3)
    ag(1, 1, 0)
    V_(0, 2)
    V_(0, 3)
    ag(1, 1, 1)
    GV(0, 0)
    transpose(tokT, tokb)
    GV(0, 1)
    ag(1, 2, 0)
    GU(0, 0)
    transpose(w1T, w1)
    ag(1, 2, 1)
    GU(0, 1)
    c_up.wait()
    a2a_wait(upb, 1, a2a_recv)
    P_(1, 0)
    P_(1, 1)
    transpose(upT, upb)
    GS(0, 0)
    grad_mm(0, 0)
    grad_mm(0, 1)
    S_(1, 0)
    P_(1, 2)
    GS(0, 1)
    grad_mm(0, 3)
    grad_mm(0, 2)
    RS(0, 0)
    S_(1, 1)
    ag(1, 3, 0)
    ag(1, 3, 1)
    P_(1, 3)
    S_(1, 2)
    U_(1, 0)
    S_(1, 3)
    U_(1, 1)
    V_(1, 0)
    RS(0, 1)
    U_(1, 2)
    V_(1, 1)
    U_(1, 3)
    V_(1, 2)
    V_(1, 3)
    GV(1, 0)
    RS(0, 2)
    GV(1, 1)
    GU(1, 0)
    RS(0, 3)
    GU(1, 1)
    GS(1, 0)
    GS(1, 1)
    for c in range(NT - 1, max(NT - 3, -1), -1):
        grad_mm(1, c)
    RS(1, 0)
    for c in range(NT - 2):
        grad_mm(1, c)
    tg_mm(0, 2)
    RS(1, 1)
    tg_mm(2, 4)
    tg_start()
    RS_end(0)
    c_o = pltpu.make_async_copy(res.at[0], outg_out, loc_sem.at[0])
    c_o.start()
    RS(1, 2)
    drain()
    a2a_wait(tokb, 0, a2a_send)
    a2a_wait(upb, 1, a2a_send)
    RS(1, 3)
    tg_end()
    c_t = pltpu.make_async_copy(tga, tg_out, loc_sem.at[1])
    c_t.start()
    RS_end(1)
    c_i = pltpu.make_async_copy(res.at[1], ing_out, loc_sem.at[2])
    c_i.start()
    drain()
    a2a_wait(tgb, 2, a2a_send)
    c_o.wait()
    c_t.wait()
    c_i.wait()


def finish(tg, ing, outg, tg_o, ing_o, outg_o, tb, tf, ob, ot, sem):
    NC = 4
    D = tb.shape[1]
    C = D // NC
    c_o = pltpu.make_async_copy(outg, ob, sem.at[0])
    c_o.start()
    c_i = pltpu.make_async_copy(ing, ing_o, sem.at[1])
    c_i.start()
    ins = [pltpu.make_async_copy(tg.at[:, pl.ds(C * c, C)], tb.at[:, pl.ds(C * c, C)], sem.at[2 + c]) for c in range(NC)]
    for c in ins:
        c.start()
    outs = []
    for n in range(NC):
        ins[n].wait()
        cols = pl.ds(C * n, C)
        tf[:, cols] = tb[:, cols].astype(F32)
        o = pltpu.make_async_copy(tf.at[:, cols], tg_o.at[:, cols], sem.at[2 + NC + n])
        o.start()
        outs.append(o)
    c_o.wait()
    ot[...] = ob[...].T
    o = pltpu.make_async_copy(ot, outg_o, sem.at[2 + 2 * NC])
    o.start()
    outs.append(o)
    c_i.wait()
    for o in outs:
        o.wait()


def make(mesh):
    NXL, NDP, NZ = mesh.shape["dcn"], mesh.shape["dp"], mesh.shape["tp"]
    NP = NXL * NDP
    NS = 1
    while NS * NS * 2 < NP:
        NS += 1

    def per_device(tokens, upstream, w_in, w_out):
        T, D = tokens.shape
        B = D // NP
        W = B + 64
        HID = 128 * NZ
        H = NZ // 2
        R = NP * T
        HR = R // 2
        UR = HR // NS
        cfg = (NXL, NDP, NZ, NS, T, B, W, HID)
        NQ = 4 * (HID // min(256, HID))
        DMA = pltpu.SemaphoreType.DMA
        scratch = [
            pltpu.VMEM((R, W), BF16),
            pltpu.VMEM((R, W), BF16),
            pltpu.VMEM((W, R), BF16),
            pltpu.VMEM((W, R), BF16),
            pltpu.VMEM((W, HID), BF16),
            pltpu.VMEM((W, HID), BF16),
            pltpu.VMEM((HID, W), BF16),
            pltpu.VMEM((128, W), BF16),
            pltpu.VMEM((2, R, HID), F32),
            pltpu.VMEM((2, HR, HID), F32),
            pltpu.VMEM((2, NS - 1, UR, HID), F32),
            pltpu.VMEM((2, UR, HID), F32),
            pltpu.VMEM((2, NS - 1, T, HID), F32),
            pltpu.VMEM((T, HID), F32),
            pltpu.VMEM((2, R, HID), BF16),
            pltpu.VMEM((2, W, HID), F32),
            pltpu.VMEM((4 * H, B, 128), BF16),
            pltpu.VMEM((4 * H, B, 128), BF16),
            pltpu.VMEM((R, W), BF16),
            pltpu.VMEM((R, W), BF16),
            pltpu.VMEM((T, D), BF16),
            pltpu.VMEM((2, B, 128), F32),
            DMA((4,)),
            DMA((3,)),
            DMA((3,)),
            DMA((8 * H,)),
            DMA((8 * H,)),
            DMA((8 * H,)),
            DMA((8 * H,)),
            DMA((NQ,)),
            DMA((NQ,)),
            DMA((NQ, NS - 1)),
            DMA((NQ, NS - 1)),
            DMA((NQ, NS - 1)),
            DMA((NQ, NS - 1)),
        ]
        tg, ing, outg = pl.pallas_call(
            functools.partial(kernel, cfg),
            out_shape=(
                jax.ShapeDtypeStruct((T, D), BF16),
                jax.ShapeDtypeStruct((B, 128), F32),
                jax.ShapeDtypeStruct((B, 128), F32),
            ),
            in_specs=[pl.BlockSpec(memory_space=pl.ANY)] * 4,
            out_specs=tuple([pl.BlockSpec(memory_space=pl.ANY)] * 3),
            scratch_shapes=scratch,
            compiler_params=pltpu.CompilerParams(
                collective_id=0, has_side_effects=True, vmem_limit_bytes=56 * 2**20
            ),
        )(tokens, upstream, w_in, w_out)
        return pl.pallas_call(
            finish,
            out_shape=(
                jax.ShapeDtypeStruct((T, D), F32),
                jax.ShapeDtypeStruct((B, 128), F32),
                jax.ShapeDtypeStruct((128, B), F32),
            ),
            in_specs=[pl.BlockSpec(memory_space=pl.ANY)] * 3,
            out_specs=tuple([pl.BlockSpec(memory_space=pl.ANY)] * 3),
            scratch_shapes=[
                pltpu.VMEM((T, D), BF16),
                pltpu.VMEM((T, D), F32),
                pltpu.VMEM((B, 128), F32),
                pltpu.VMEM((128, B), F32),
                DMA((11,)),
            ],
            compiler_params=pltpu.CompilerParams(vmem_limit_bytes=16 * 2**20),
        )(tg, ing, outg)

    return per_device


def solution(mesh):
    placed = (
        P(("dcn", "dp", "tp"), None),
        P(("dcn", "dp", "tp"), None),
        P(None, "tp"),
        P("tp", None),
    )
    return jax.shard_map(
        make(mesh),
        mesh=mesh,
        in_specs=placed,
        out_specs=(P(("dcn", "dp", "tp"), None), P(("dcn", "dp"), "tp"), P("tp", ("dcn", "dp"))),
        check_vma=False,
    )
```

```python
import functools

import jax
import jax.numpy as jnp
from jax import lax
from jax.experimental import pallas as pl
from jax.experimental.pallas import tpu as pltpu
from jax.sharding import PartitionSpec as P

MESH = pl.DeviceIdType.MESH
F32 = jnp.float32
BF16 = jnp.bfloat16


def mult(value, of):
    return pl.multiple_of(value, of)


def kernel(
    cfg,
    tokens, upstream, w_in, w_out,
    tg_out, ing_out, outg_out,
    tokb, upb, tokT, upT, w1, w2, w1T, wo_tmp,
    prep, sibr, urecv, usum, vrecv, pos, gath,
    grad, zsend, zrecv, tgb, tgr, tga, res,
    loc_sem, a2a_send, a2a_recv, ag_send, ag_recv, rs_send, rs_recv,
    sib_send, sib_recv, u_send, u_recv, v_send, v_recv,
):
    NXL, NDP, NZ, NS, T, B, W, HID = cfg
    NP = NXL * NDP
    H = NZ // 2
    R = NP * T
    HR = R // 2
    HB = B // 2
    AP0 = 4 if B % 64 == 0 else 2
    TS = min(256, HID)
    NT = HID // TS

    z = lax.axis_index("tp")
    dcn = lax.axis_index("dcn")
    dp = lax.axis_index("dp")
    k = dp % 2
    y = (dp // 2) % NS
    x = (dp // (2 * NS)) * NXL + dcn
    me = dcn * NDP + dp
    u = jnp.where(k == 0, x, y)
    v = jnp.where(k == 0, y, x)

    def dev(x_, y_, k_):
        return (x_ % NXL, (x_ // NXL) * (2 * NS) + y_ * 2 + k_, z)

    def dev_i(i_):
        return (i_ // NDP, i_ % NDP, z)

    sib = dev(x, y, 1 - k)

    def u_peer(u_):
        return dev(jnp.where(k == 0, u_, x), jnp.where(k == 0, y, u_), k)

    def v_peer(v_):
        return dev(jnp.where(k == 0, x, v_), jnp.where(k == 0, v_, y), k)

    right = (dcn, dp, (z + 1) % NZ)
    left = (dcn, dp, (z + NZ - 1) % NZ)
    zn = (right, left)

    def lane0(i_):
        return mult(128 * ((B // 64) * (i_ // 2) + (B // 128) * (i_ % 2)), 128)

    row0 = mult(64 * k, 64)
    pad0 = mult(jnp.where(k == 0, B, 0), 64)
    sends = []

    def send(src, dst, ss, rs, to):
        c = pltpu.make_async_remote_copy(
            src_ref=src, dst_ref=dst, send_sem=ss, recv_sem=rs, device_id=to, device_id_type=MESH
        )
        c.start()
        sends.append(c)
        return c

    def landed(ref, sem):
        pltpu.make_async_copy(ref, ref, sem).wait()

    def drain(keep=0):
        while len(sends) > keep:
            sends.pop(0).wait_send()

    def slot(m):
        if abs(m) == H:
            return NZ - 1
        return 2 * m if m >= 0 else -2 * m - 1

    def lanes(s):
        return pl.ds(128 * s, 128)

    barrier = pltpu.get_barrier_semaphore()
    my_lane = lane0(me)
    my_rows = pl.ds(mult(T * me, T), T)

    def entry():
        pl.semaphore_signal(barrier, inc=1, device_id=right, device_id_type=MESH)
        if NZ > 2:
            pl.semaphore_signal(barrier, inc=1, device_id=left, device_id_type=MESH)

        @pl.loop(1, NP)
        def _(d):
            pl.semaphore_signal(barrier, inc=1, device_id=dev_i((me + d) % NP), device_id_type=MESH)

    c_win = pltpu.make_async_copy(
        w_in.at[pl.ds(mult(B * me, 64), B), :], w1.at[pl.ds(row0, B), lanes(0)], loc_sem.at[0]
    )
    c_wout = pltpu.make_async_copy(w_out.at[:, pl.ds(my_lane, W)], wo_tmp, loc_sem.at[1])
    c_tok = pltpu.make_async_copy(tokens.at[:, pl.ds(my_lane, W)], tokb.at[my_rows, :], loc_sem.at[2])
    c_up = pltpu.make_async_copy(upstream.at[:, pl.ds(my_lane, W)], upb.at[my_rows, :], loc_sem.at[3])

    def entry_wait():
        c_win.wait()
        pl.semaphore_wait(barrier, NP + (1 if NZ > 2 else 0))

    def own_wout():
        w1[pl.ds(pad0, 64), :] = jnp.zeros((64, HID), BF16)
        w2[pl.ds(pad0, 64), :] = jnp.zeros((64, HID), BF16)
        c_wout.wait()
        w2[pl.ds(row0, B), lanes(0)] = jnp.where(k == 0, wo_tmp[:, 0:B].T, wo_tmp[:, W - B : W].T)

    def part(hf, np_=2):
        return pl.ds(mult(row0 + (B // np_) * hf, 16), B // np_)

    AP = (AP0, 2)

    def ag_parts(wi, step, d):
        np_ = AP[wi]
        if step < H - 1:
            return range(np_)
        return range(np_ // 2) if d == 0 else range(np_ // 2, np_)

    def ag_sem(wi, step, d, hf):
        return ((wi * 2 + d) * H + step) * 4 + hf

    def ag_send_one(wi, step, d, hf):
        w = (w1, w2)[wi]
        sg = 1 if d else -1
        n = ag_sem(wi, step, d, hf)
        rows = part(hf, AP[wi])
        send(
            w.at[rows, lanes(slot(sg * step))], w.at[rows, lanes(slot(sg * (step + 1)))],
            ag_send.at[n], ag_recv.at[n], zn[d],
        )

    def ag_start(wi):
        for hf in range(AP[wi]):
            for d in (0, 1):
                if hf in ag_parts(wi, 0, d):
                    ag_send_one(wi, 0, d, hf)

    def ag(wi, step, half):
        if step >= H:
            return
        w = (w1, w2)[wi]
        np_ = AP[wi]
        for hf in range(np_ // 2 * half, np_ // 2 * (half + 1)):
            for d in (0, 1):
                if hf in ag_parts(wi, step, d):
                    n = ag_sem(wi, step, d, hf)
                    landed(w.at[part(hf, np_), lanes(slot((1 if d else -1) * (step + 1)))], ag_recv.at[n])
                    if step + 1 < H and hf in ag_parts(wi, step + 1, d):
                        ag_send_one(wi, step + 1, d, hf)

    def a2a_start(src, dst, n, lo, hi):
        @pl.loop(lo, hi)
        def _(dd):
            to = (me + dd) % NP
            pltpu.make_async_remote_copy(
                src_ref=src.at[:, pl.ds(lane0(to), W)],
                dst_ref=dst.at[my_rows, :],
                send_sem=a2a_send.at[n],
                recv_sem=a2a_recv.at[n],
                device_id=dev_i(to),
                device_id_type=MESH,
            ).start()

    def a2a_wait(buf, n, sems):
        landed(buf.at[pl.ds(0, R - T), :], sems.at[n])

    my_half = mult(HR * k, HR)
    sib_half = mult(HR * (1 - k), HR)
    UR = HR // NS
    mine = pl.ds(mult(my_half + UR * u + T * v, T), T)
    pend = {}

    def chunk(c):
        return pl.ds(TS * c, TS)

    def tiles(c):
        return [pl.ds(TS * c + t, min(256, TS)) for t in range(0, TS, min(256, TS))]

    def mm_part(n, c, start):
        lhs, w = ((tokb, w1), (upb, w2))[n]
        for cols in tiles(c):
            prep[n, pl.ds(start, HR), cols] = jnp.dot(
                lhs[pl.ds(start, HR), :], w[:, cols], preferred_element_type=F32
            )

    def P_(n, c):
        if c >= NT:
            return
        q = n * NT + c
        mm_part(n, c, sib_half)
        pend["s", n, c] = send(
            prep.at[n, pl.ds(sib_half, HR), chunk(c)], sibr.at[n, :, chunk(c)], sib_send.at[q], sib_recv.at[q], sib
        )
        mm_part(n, c, my_half)

    def S_(n, c):
        if c >= NT:
            return
        q = n * NT + c
        pend["s", n, c].wait_recv()
        out = []
        for r in [2, 1, 3, 0] if NS == 4 else list(range(1, NS)) + [0]:
            uu = (u + r) % NS
            rows = pl.ds(mult(my_half + UR * uu, UR), UR)
            prep[n, rows, chunk(c)] += sibr[n, pl.ds(mult(UR * uu, UR), UR), chunk(c)]
            if r:
                out.append(
                    send(
                        prep.at[n, rows, chunk(c)], urecv.at[n, r - 1, :, chunk(c)],
                        u_send.at[q, r - 1], u_recv.at[q, r - 1], u_peer(uu),
                    )
                )
        pend["u", n, c] = out

    def U_(n, c):
        if c >= NT:
            return
        q = n * NT + c
        for d in pend["u", n, c]:
            d.wait_recv()
        tot = prep[n, pl.ds(mult(my_half + UR * u, UR), UR), chunk(c)]
        for r in range(NS - 1):
            tot = tot + urecv[n, r, :, chunk(c)]
        usum[n, :, chunk(c)] = tot
        pend["v", n, c] = [
            send(
                usum.at[n, pl.ds(mult(T * ((v + r) % NS), T), T), chunk(c)], vrecv.at[n, r - 1, :, chunk(c)],
                v_send.at[q, r - 1], v_recv.at[q, r - 1], v_peer((v + r) % NS),
            )
            for r in range(1, NS)
        ]

    def V_(n, c):
        if c >= NT:
            return
        for d in pend["v", n, c]:
            d.wait_recv()
        tot = usum[n, pl.ds(mult(T * v, T), T), chunk(c)]
        for r in range(NS - 1):
            tot = tot + vrecv[n, r, :, chunk(c)]
        if n == 0:
            positive = jnp.maximum(tot, 0.0)
            pos[:, chunk(c)] = positive
            gath[0, mine, chunk(c)] = (positive * positive).astype(BF16)
        else:
            gath[1, mine, chunk(c)] = (tot * 2.0 * pos[:, chunk(c)]).astype(BF16)
        if (c + 1) % CG == 0:
            GV0(n, c // CG)

    CG = 1
    NG = NT // CG

    def group(g):
        return pl.ds(TS * CG * g, TS * CG)

    def gq(n, g):
        return 2 * NT + n * NG + g

    def GV0(n, g):
        ref = gath.at[n, mine, group(g)]
        pend["gv", n, g] = [
            send(ref, ref, v_send.at[gq(n, g), r - 1], v_recv.at[gq(n, g), r - 1], v_peer((v + r) % NS))
            for r in range(1, NS)
        ]

    def GV(n, g):
        if g >= NG:
            return
        for d in pend["gv", n, g]:
            d.wait_recv()
        ref = gath.at[n, pl.ds(mult(my_half + UR * u, UR), UR), group(g)]
        pend["gu", n, g] = [
            send(ref, ref, u_send.at[gq(n, g), r - 1], u_recv.at[gq(n, g), r - 1], u_peer((u + r) % NS))
            for r in range(1, NS)
        ]

    def GU(n, g):
        if g >= NG:
            return
        for d in pend["gu", n, g]:
            d.wait_recv()
        ref = gath.at[n, pl.ds(my_half, HR), group(g)]
        pend["gs", n, g] = send(ref, ref, sib_send.at[gq(n, g)], sib_recv.at[gq(n, g)], sib)

    def GS(n, g):
        if g >= NG:
            return
        pend["gs", n, g].wait_recv()

    MT = W // 2

    def grad_mm(n, c):
        if c >= NT:
            return
        lhsT = (upT, tokT)[n]

        @pl.loop(0, 2)
        def _(m):
            rows = pl.ds(mult(MT * m, MT), MT)
            for cols in tiles(c):
                grad[n, rows, cols] = jnp.dot(lhsT[rows, :], gath[n, :, cols], preferred_element_type=F32)

    def rs_dest(d, step):
        m = H - step
        return slot(m) if d == 0 else slot(-m)

    def rs_halves(step, d):
        return (d,) if step == 0 else (0, 1)

    def rs_get(n, d, step, hf):
        q = (n * 2 + d) * H + step
        rows = pl.ds(HB * hf, HB)
        landed(zrecv.at[q, rows, :], rs_recv.at[q * 2 + hf])
        return zrecv[q, rows, :].astype(F32)

    def rs_one(n, step, d, hf):
        q = (n * 2 + d) * H + step
        val = grad[n, part(hf), lanes(rs_dest(d, step))]
        if step >= 1 and hf in rs_halves(step - 1, d):
            val = val + rs_get(n, d, step - 1, hf)
        rows = pl.ds(HB * hf, HB)
        zsend[q, rows, :] = val.astype(BF16)
        send(
            zsend.at[q, rows, :], zrecv.at[q, rows, :],
            rs_send.at[q * 2 + hf], rs_recv.at[q * 2 + hf], zn[d],
        )

    def RS(n, step):
        if step >= H:
            return
        if step == 0:
            rs_one(n, 0, 0, 0)
            rs_one(n, 0, 1, 1)
            if H > 1:
                rs_one(n, 1, 0, 1)
                rs_one(n, 1, 1, 0)
        elif step == 1:
            rs_one(n, 1, 0, 0)
            rs_one(n, 1, 1, 1)
        else:
            rs_one(n, step, 0, 1)
            rs_one(n, step, 1, 0)
            rs_one(n, step, 0, 0)
            rs_one(n, step, 1, 1)

    def RS_end(n):
        for hf in (0, 1):
            val = grad[n, part(hf), lanes(0)]
            for d in (0, 1):
                if hf in rs_halves(H - 1, d):
                    val = val + rs_get(n, d, H - 1, hf)
            res[n, pl.ds(HB * hf, HB), :] = val

    def tg_mm(lo, hi):
        @pl.loop(lo * R // 4 // TR, hi * R // 4 // TR)
        def _(t):
            rows = pl.ds(mult(TR * t, TR), TR)
            tgb[rows, :] = jnp.dot(gath[1, rows, :], w1T[...], preferred_element_type=F32).astype(BF16)

    TR = min(128, R // 4)

    def tg_start():
        @pl.loop(1, NP)
        def _(dd):
            to = (me + dd) % NP
            pltpu.make_async_remote_copy(
                src_ref=tgb.at[pl.ds(mult(T * to, T), T), :],
                dst_ref=tgr.at[my_rows, :],
                send_sem=a2a_send.at[2],
                recv_sem=a2a_recv.at[2],
                device_id=dev_i(to),
                device_id_type=MESH,
            ).start()

        tgr[my_rows, :] = tgb[my_rows, :]

    FT = (B // 128) * 128

    def tg_end():
        a2a_wait(tgr, 2, a2a_recv)

        @pl.loop(0, NP // 2)
        def _(p):
            base = 2 * B * p
            r0 = pl.ds(mult(2 * T * p, 2 * T), T)
            r1 = pl.ds(mult(2 * T * p + T, T), T)
            tga[:, pl.ds(mult(base, 128), FT)] = tgr[r0, 0:FT]
            tga[:, pl.ds(mult(base + FT, 128), 128)] = tgr[r0, FT:W] + tgr[r1, 0:128]
            tga[:, pl.ds(mult(base + FT + 128, 128), FT)] = tgr[r1, 128:W]

    def transpose(dst, src):
        dst[...] = src[...].T

    entry()
    for c in (c_win, c_wout, c_tok, c_up):
        c.start()
    entry_wait()
    ag_start(0)
    a2a_start(tokens, tokb, 0, 1, NP)
    a2a_start(upstream, upb, 1, 1, NP // 2)
    a2a_start(upstream, upb, 1, NP // 2, NP)
    own_wout()
    ag_start(1)
    ag(0, 0, 0)
    ag(0, 0, 1)
    ag(1, 0, 0)
    ag(0, 1, 0)
    c_tok.wait()
    a2a_wait(tokb, 0, a2a_recv)
    P_(0, 0)
    ag(0, 1, 1)
    ag(1, 0, 1)
    P_(0, 1)
    S_(0, 0)
    S_(0, 1)
    transpose(tokT, tokb)
    ag(1, 1, 0)
    ag(0, 2, 0)
    ag(0, 2, 1)
    P_(0, 2)
    ag(1, 1, 1)
    c_up.wait()
    a2a_wait(upb, 1, a2a_recv)
    S_(0, 2)
    P_(1, 1)
    ag(1, 2, 0)
    ag(0, 3, 1)
    U_(0, 0)
    U_(0, 1)
    ag(0, 3, 0)
    P_(0, 3)
    S_(1, 1)
    P_(1, 0)
    ag(1, 2, 1)
    P_(1, 2)
    ag(1, 3, 1)
    S_(0, 3)
    ag(1, 3, 0)
    P_(1, 3)
    U_(0, 2)
    S_(1, 2)
    S_(1, 3)
    U_(0, 3)
    V_(0, 2)
    S_(1, 0)
    U_(1, 2)
    V_(0, 1)
    V_(0, 0)
    U_(1, 1)
    U_(1, 3)
    V_(0, 3)
    GV(0, 2)
    U_(1, 0)
    V_(1, 2)
    GV(0, 0)
    V_(1, 3)
    GV(0, 3)
    V_(1, 1)
    GV(0, 1)
    transpose(w1T, w1)
    V_(1, 0)
    GU(0, 2)
    GV(1, 2)
    GV(1, 3)
    GU(0, 3)
    transpose(upT, upb)
    GV(1, 1)
    GS(0, 2)
    GV(1, 0)
    GU(0, 1)
    grad_mm(0, 2)
    GS(0, 3)
    grad_mm(0, 3)
    RS(0, 0)
    GU(1, 2)
    GU(1, 3)
    GU(1, 1)
    GU(0, 0)
    GS(1, 2)
    grad_mm(1, 2)
    GS(1, 3)
    grad_mm(1, 3)
    GS(0, 1)
    GU(1, 0)
    RS(1, 0)
    RS(0, 1)
    GS(1, 1)
    GS(0, 0)
    GS(1, 0)
    tg_mm(0, 4)
    tg_start()
    RS(1, 1)
    grad_mm(0, 1)
    grad_mm(1, 0)
    grad_mm(0, 0)
    drain(40)
    RS(0, 2)
    grad_mm(1, 1)
    drain(40)
    RS(1, 2)
    RS(0, 3)
    drain(40)
    RS(1, 3)
    RS_end(0)
    c_o = pltpu.make_async_copy(res.at[0], outg_out, loc_sem.at[0])
    c_o.start()
    tg_end()
    c_t = pltpu.make_async_copy(tga, tg_out, loc_sem.at[1])
    c_t.start()
    RS_end(1)
    c_i = pltpu.make_async_copy(res.at[1], ing_out, loc_sem.at[2])
    c_i.start()
    a2a_wait(tokb, 0, a2a_send)
    a2a_wait(upb, 1, a2a_send)
    drain()
    a2a_wait(tgb, 2, a2a_send)
    c_o.wait()
    c_t.wait()
    c_i.wait()


def finish(tg, ing, outg, tg_o, ing_o, outg_o, tb, tf, sem):
    NC = 4
    D = tb.shape[1]
    C = D // NC
    c_o = pltpu.make_async_copy(outg, outg_o, sem.at[0])
    c_o.start()
    c_i = pltpu.make_async_copy(ing, ing_o, sem.at[1])
    c_i.start()
    ins = [pltpu.make_async_copy(tg.at[:, pl.ds(C * c, C)], tb.at[:, pl.ds(C * c, C)], sem.at[2 + c]) for c in range(NC)]
    for c in ins:
        c.start()
    outs = []
    for n in range(NC):
        ins[n].wait()
        cols = pl.ds(C * n, C)
        tf[:, cols] = tb[:, cols].astype(F32)
        o = pltpu.make_async_copy(tf.at[:, cols], tg_o.at[:, cols], sem.at[2 + NC + n])
        o.start()
        outs.append(o)
    c_o.wait()
    c_i.wait()
    for o in outs:
        o.wait()


def make(mesh):
    NXL, NDP, NZ = mesh.shape["dcn"], mesh.shape["dp"], mesh.shape["tp"]
    NP = NXL * NDP
    NS = 1
    while NS * NS * 2 < NP:
        NS += 1

    def per_device(tokens, upstream, w_in, w_out):
        T, D = tokens.shape
        B = D // NP
        W = B + 64
        HID = 128 * NZ
        H = NZ // 2
        R = NP * T
        HR = R // 2
        UR = HR // NS
        cfg = (NXL, NDP, NZ, NS, T, B, W, HID)
        NQ = 4 * (HID // min(256, HID))
        DMA = pltpu.SemaphoreType.DMA
        scratch = [
            pltpu.VMEM((R, W), BF16),
            pltpu.VMEM((R, W), BF16),
            pltpu.VMEM((W, R), BF16),
            pltpu.VMEM((W, R), BF16),
            pltpu.VMEM((W, HID), BF16),
            pltpu.VMEM((W, HID), BF16),
            pltpu.VMEM((HID, W), BF16),
            pltpu.VMEM((128, W), BF16),
            pltpu.VMEM((2, R, HID), F32),
            pltpu.VMEM((2, HR, HID), F32),
            pltpu.VMEM((2, NS - 1, UR, HID), F32),
            pltpu.VMEM((2, UR, HID), F32),
            pltpu.VMEM((2, NS - 1, T, HID), F32),
            pltpu.VMEM((T, HID), F32),
            pltpu.VMEM((2, R, HID), BF16),
            pltpu.VMEM((2, W, HID), F32),
            pltpu.VMEM((4 * H, B, 128), BF16),
            pltpu.VMEM((4 * H, B, 128), BF16),
            pltpu.VMEM((R, W), BF16),
            pltpu.VMEM((R, W), BF16),
            pltpu.VMEM((T, D), BF16),
            pltpu.VMEM((2, B, 128), F32),
            DMA((4,)),
            DMA((3,)),
            DMA((3,)),
            DMA((16 * H,)),
            DMA((16 * H,)),
            DMA((8 * H,)),
            DMA((8 * H,)),
            DMA((NQ,)),
            DMA((NQ,)),
            DMA((NQ, NS - 1)),
            DMA((NQ, NS - 1)),
            DMA((NQ, NS - 1)),
            DMA((NQ, NS - 1)),
        ]
        tg, ing, outg = pl.pallas_call(
            functools.partial(kernel, cfg),
            out_shape=(
                jax.ShapeDtypeStruct((T, D), BF16),
                jax.ShapeDtypeStruct((B, 128), F32),
                jax.ShapeDtypeStruct((B, 128), F32),
            ),
            in_specs=[pl.BlockSpec(memory_space=pltpu.HBM)] * 4,
            out_specs=tuple([pl.BlockSpec(memory_space=pl.ANY)] * 3),
            scratch_shapes=scratch,
            compiler_params=pltpu.CompilerParams(
                collective_id=0, has_side_effects=True, vmem_limit_bytes=105 * 2**19
            ),
        )(tokens, upstream, w_in, w_out)
        tg_f, ing_f, outg_f = pl.pallas_call(
            finish,
            out_shape=(
                jax.ShapeDtypeStruct((T, D), F32),
                jax.ShapeDtypeStruct((B, 128), F32),
                jax.ShapeDtypeStruct((B, 128), F32),
            ),
            in_specs=[pl.BlockSpec(memory_space=pl.ANY)] * 3,
            out_specs=tuple([pl.BlockSpec(memory_space=pl.ANY)] * 3),
            scratch_shapes=[
                pltpu.VMEM((T, D), BF16),
                pltpu.VMEM((T, D), F32),
                DMA((10,)),
            ],
            compiler_params=pltpu.CompilerParams(vmem_limit_bytes=50 * 2**20),
        )(tg, ing, outg)
        return tg_f, ing_f, outg_f.T

    return per_device


def solution(mesh):
    placed = (
        P(("dcn", "dp", "tp"), None),
        P(("dcn", "dp", "tp"), None),
        P(None, "tp"),
        P("tp", None),
    )
    return jax.shard_map(
        make(mesh),
        mesh=mesh,
        in_specs=placed,
        out_specs=(P(("dcn", "dp", "tp"), None), P(("dcn", "dp"), "tp"), P("tp", ("dcn", "dp"))),
        check_vma=False,
    )
```

```python
import functools

import jax
import jax.numpy as jnp
from jax import lax
from jax.experimental import pallas as pl
from jax.experimental.pallas import tpu as pltpu
from jax.sharding import PartitionSpec as P

MESH = pl.DeviceIdType.MESH
F32 = jnp.float32
BF16 = jnp.bfloat16


def mult(value, of):
    return pl.multiple_of(value, of)


def kernel(
    cfg,
    tokens, upstream, w_in, w_out,
    tg_out, ing_out, outg_out,
    tokb, upb, tokT, upT, own1, own2, w1, w2, w1T, wo_tmp,
    prep, urecv, usum, vrecv, pos, gath,
    grad, ownp, zsend, zrecv, zfin, tgp, tgx, tgb, res,
    loc_sem, a2a_send, a2a_recv, f_send, f_recv, ag_sent, ag_recv, rs_sent, rs_recv,
    fin_sent, fin_recv, u_send, u_recv, v_send, v_recv,
):
    NXL, NDP, NZ, NS, T, B = cfg
    NP = NXL * NDP
    NC = NP // 2
    H = NZ // 2
    BC = 2 * B
    R = NP * T
    RC = R // 2
    UR = R // NS
    VR = UR // NS
    HP = B // 2

    z = lax.axis_index("tp")
    dcn = lax.axis_index("dcn")
    dp = lax.axis_index("dp")
    k = dp % 2
    y = (dp // 2) % NS
    x = (dp // (2 * NS)) * NXL + dcn
    p = (dcn * NDP + dp) // 2
    u = jnp.where(k == 0, x, y)
    v = jnp.where(k == 0, y, x)
    up = (z + 1) % NZ
    down = (z + NZ - 1) % NZ

    def dev(x_, y_, k_):
        return (x_ % NXL, (x_ // NXL) * (2 * NS) + y_ * 2 + k_, z)

    def chip(p_):
        i_ = 2 * p_ + k
        return (i_ // NDP, i_ % NDP, z)

    def at_z(z_, k_):
        return (dcn, dp - k + k_, z_)

    sib = dev(x, y, 1 - k)

    def u_peer(u_):
        return dev(jnp.where(k == 0, u_, x), jnp.where(k == 0, y, u_), k)

    def v_peer(v_):
        return dev(jnp.where(k == 0, x, v_), jnp.where(k == 0, v_, y), k)

    ag_z = jnp.where(k == 0, up, down)
    rs_z = jnp.where(k == 0, down, up)

    sends = []

    def send(src, dst, ss, rs, to, when=None):
        c = pltpu.make_async_remote_copy(
            src_ref=src, dst_ref=dst, send_sem=ss, recv_sem=rs, device_id=to, device_id_type=MESH
        )
        if when is None:
            c.start()
        else:
            pl.when(when)(c.start)
        sends.append((when, c))
        return c

    def landed(ref, sem):
        pltpu.make_async_copy(ref, ref, sem).wait()

    def drain(keep=0):
        while len(sends) > keep:
            when, c = sends.pop(0)
            if when is None:
                c.wait_send()
            else:
                pl.when(when)(c.wait_send)

    LAST = H - 1

    def lanes(c, n=1):
        return pl.ds(128 * c, 128 * n)

    barrier = pltpu.get_barrier_semaphore()
    cols = pl.ds(mult(BC * p, 128), BC)
    my_tok = pl.ds(mult(RC * k + T * p, T), T)
    my_half = pl.ds(mult(RC * k, RC), RC)
    sib_half = pl.ds(mult(RC * (1 - k), RC), RC)

    def entry():
        for z_ in (up, down) if NZ > 2 else (up,):
            for k_ in (0, 1):
                pl.semaphore_signal(barrier, inc=1, device_id=at_z(z_, k_), device_id_type=MESH)
        pl.semaphore_signal(barrier, inc=1, device_id=sib, device_id_type=MESH)

        @pl.loop(1, NC)
        def _(d):
            pl.semaphore_signal(barrier, inc=1, device_id=chip((p + d) % NC), device_id_type=MESH)

    c_win = pltpu.make_async_copy(w_in.at[pl.ds(mult(BC * p, 128), BC), :], own1, loc_sem.at[0])
    c_wout = pltpu.make_async_copy(w_out.at[:, cols], wo_tmp, loc_sem.at[1])
    c_tok = pltpu.make_async_copy(tokens.at[:, cols], tokb.at[my_tok, :], loc_sem.at[2])
    c_up = pltpu.make_async_copy(upstream.at[:, cols], upb.at[my_tok, :], loc_sem.at[3])

    def entry_wait():
        c_win.wait()
        pl.semaphore_wait(barrier, NC + (4 if NZ > 2 else 2))

    def own_wout():
        c_wout.wait()
        own2[...] = wo_tmp[...].T

        @pl.when(k == 0)
        def _():
            w1[:, lanes(LAST)] = own1[...]
            w2[:, lanes(LAST)] = own2[...]

    def rows_at(q):
        return pl.ds(HP * q, HP)

    def ag_block(wi, step):
        return (own1, own2)[wi] if step == 0 else (w1, w2)[wi].at[:, lanes(step - 1)]

    def ag_sem(wi, step, q):
        return (wi * H + step) * 4 + q

    def ag_send(wi, step, q):
        w = (w1, w2)[wi]
        n = ag_sem(wi, step, q)
        src = ag_block(wi, step).at[rows_at(q), :]
        if step < H - 1:
            send(src, w.at[rows_at(q), lanes(step)], ag_sent.at[n], ag_recv.at[n], at_z(ag_z, k))
        else:
            send(
                src, w.at[rows_at(q), lanes(LAST)], ag_sent.at[n], ag_recv.at[n], at_z(ag_z, 1),
                when=k == q // 2,
            )


    def ag_start(wi):
        for q in range(4):
            ag_send(wi, 0, q)

    def ag(wi, step, half):
        w = (w1, w2)[wi]
        for q in (2 * half, 2 * half + 1):
            arrived = w.at[rows_at(q), lanes(step)]
            if step < H - 1:
                landed(arrived, ag_recv.at[ag_sem(wi, step, q)])
                ag_send(wi, step + 1, q)
            else:
                pl.when(k == 1)(functools.partial(landed, arrived, ag_recv.at[ag_sem(wi, step, q)]))

    def a2a_start(src, dst, n):
        @pl.loop(1, NC)
        def _(d):
            to = (p + d) % NC
            pltpu.make_async_remote_copy(
                src_ref=src.at[:, pl.ds(mult(BC * to, 128), BC)],
                dst_ref=dst.at[my_tok, :],
                send_sem=a2a_send.at[n],
                recv_sem=a2a_recv.at[n],
                device_id=chip(to),
                device_id_type=MESH,
            ).start()

    def a2a_wait(n, sems):
        landed(tokb.at[pl.ds(0, RC - T), :], sems.at[n])

    def A2F(n):
        (c_tok, c_up)[n].wait()
        a2a_wait(n, a2a_recv)
        ref = (tokb, upb)[n].at[my_half, :]
        send(ref, ref, f_send.at[n], f_recv.at[n], sib)

    def A2W(n):
        landed((tokb, upb)[n].at[sib_half, :], f_recv.at[n])

    mine = pl.ds(mult(UR * u + VR * v, VR), VR)
    u_rows = pl.ds(mult(UR * u, UR), UR)
    pend = {}

    def P_(n, c, count):
        lhs, w = ((tokb, w1), (upb, w2))[n]
        prep[n, :, lanes(c, count)] = jnp.dot(lhs[...], w[:, lanes(c, count)], preferred_element_type=F32)

    def S_(n, c):
        q = n * H + c
        out = []
        for r in [2, 1, 3] if NS == 4 else range(1, NS):
            uu = (u + r) % NS
            out.append(
                send(
                    prep.at[n, pl.ds(mult(UR * uu, UR), UR), lanes(c)], urecv.at[n, r - 1, :, lanes(c)],
                    u_send.at[q, r - 1], u_recv.at[q, r - 1], u_peer(uu),
                )
            )
        pend["u", n, c] = out

    def U_(n, c):
        q = n * H + c
        for d in pend["u", n, c]:
            d.wait_recv()
        tot = prep[n, u_rows, lanes(c)]
        for r in range(NS - 1):
            tot = tot + urecv[n, r, :, lanes(c)]
        usum[n, :, lanes(c)] = tot
        pend["v", n, c] = [
            send(
                usum.at[n, pl.ds(mult(VR * ((v + r) % NS), VR), VR), lanes(c)], vrecv.at[n, r - 1, :, lanes(c)],
                v_send.at[q, r - 1], v_recv.at[q, r - 1], v_peer((v + r) % NS),
            )
            for r in range(1, NS)
        ]

    def V_(n, c):
        q = 2 * H + n * H + c
        for d in pend["v", n, c]:
            d.wait_recv()
        tot = usum[n, pl.ds(mult(VR * v, VR), VR), lanes(c)]
        for r in range(NS - 1):
            tot = tot + vrecv[n, r, :, lanes(c)]
        if n == 0:
            positive = jnp.maximum(tot, 0.0)
            pos[:, lanes(c)] = positive
            gath[0, mine, lanes(c)] = (positive * positive).astype(BF16)
        else:
            gath[1, mine, lanes(c)] = (tot * 2.0 * pos[:, lanes(c)]).astype(BF16)
        ref = gath.at[n, mine, lanes(c)]
        pend["gv", n, c] = [
            send(ref, ref, v_send.at[q, r - 1], v_recv.at[q, r - 1], v_peer((v + r) % NS)) for r in range(1, NS)
        ]

    def GV(n, c):
        q = 2 * H + n * H + c
        for d in pend["gv", n, c]:
            d.wait_recv()
        ref = gath.at[n, u_rows, lanes(c)]
        pend["gu", n, c] = [
            send(ref, ref, u_send.at[q, r - 1], u_recv.at[q, r - 1], u_peer((u + r) % NS)) for r in range(1, NS)
        ]

    def GU(n, c):
        for d in pend["gu", n, c]:
            d.wait_recv()

    def grad_mm(n, c, count):
        lhsT = (upT, tokT)[n]
        grad[n, :, lanes(c, count)] = jnp.dot(lhsT[...], gath[n, :, lanes(c, count)], preferred_element_type=F32)

    def half_rows(hf):
        return pl.ds(mult(B * hf, 64), B)

    def rs_one(n, step, hf, recv):
        q = n * H + step
        rows = half_rows(hf)
        val = grad[n, rows, lanes(H - 1 - step)]
        if recv:
            landed(zrecv.at[q - 1, rows, :], rs_recv.at[2 * (q - 1) + hf])
            val = val + zrecv[q - 1, rows, :].astype(F32)
        zsend[q, rows, :] = val.astype(BF16)
        if step < H - 1:
            send(
                zsend.at[q, rows, :], zrecv.at[q, rows, :], rs_sent.at[2 * q + hf], rs_recv.at[2 * q + hf],
                at_z(rs_z, k),
            )
        else:
            send(zsend.at[q, rows, :], zfin.at[n, k], fin_sent.at[2 * n + hf], fin_recv.at[2 * n + k], at_z(rs_z, hf))

    def RS(n, step):
        if step == 0:
            q = n * H

            @pl.when(k == 1)
            def _():
                zsend[q] = grad[n, :, lanes(LAST)].astype(BF16)

            for hf, to in ((0, at_z(up, 1)), (1, at_z(down, 0))):
                rows = pl.ds(B * hf, B)
                send(
                    zsend.at[q, rows, :], zrecv.at[q, rows, :], rs_sent.at[2 * q + hf], rs_recv.at[2 * q + hf], to,
                    when=k == 1,
                )
            rs_one(n, 1, k, False)
            send(
                grad.at[n, pl.ds(B, B), lanes(LAST)], ownp.at[n], f_send.at[2 + n], f_recv.at[2 + n], sib, when=k == 0
            )
        elif step == 1:
            rs_one(n, 1, 1 - k, True)
        else:
            rs_one(n, step, k, True)
            rs_one(n, step, 1 - k, True)

    def RS_end(n):
        for d in (0, 1):
            landed(zfin.at[n, d], fin_recv.at[2 * n + d])
        tot = zfin[n, 0].astype(F32) + zfin[n, 1].astype(F32)

        @pl.when(k == 0)
        def _():
            res[n] = tot + grad[n, 0:B, lanes(LAST)]

        @pl.when(k == 1)
        def _():
            landed(ownp.at[n], f_recv.at[2 + n])
            res[n] = tot + ownp[n]

    TR = min(128, RC)

    def tg_mm(half):
        @pl.loop(0, RC // TR)
        def _(t):
            rows = pl.ds(mult(RC * half + TR * t, TR), TR)
            tgp[rows, :] = jnp.dot(gath[1, rows, :], w1T[...], preferred_element_type=F32)

    def TG():
        tg_mm(1 - k)
        send(tgp.at[sib_half, :], tgx, f_send.at[4], f_recv.at[4], sib)
        tg_mm(k)

    c_t = pltpu.make_async_copy(tgb.at[pl.ds(mult(T * p, T), T), :], tg_out.at[:, cols], loc_sem.at[4])

    def TG2():
        landed(tgx, f_recv.at[4])

        @pl.loop(0, RC // TR)
        def _(t):
            rows = pl.ds(mult(TR * t, TR), TR)
            tgb[rows, :] = (tgp[pl.ds(mult(RC * k + TR * t, TR), TR), :] + tgx[rows, :]).astype(BF16)

        @pl.loop(1, NC)
        def _(d):
            to = (p + d) % NC
            pltpu.make_async_remote_copy(
                src_ref=tgb.at[pl.ds(mult(T * to, T), T), :],
                dst_ref=tg_out.at[:, cols],
                send_sem=a2a_send.at[2],
                recv_sem=a2a_recv.at[2],
                device_id=chip(to),
                device_id_type=MESH,
            ).start()

        c_t.start()

    def TGE():
        landed(tg_out.at[:, pl.ds(0, BC * (NC - 1))], a2a_recv.at[2])
        c_t.wait()

    def transpose(dst, src):
        dst[...] = src[...].T

    entry()
    for c in (c_win, c_wout, c_tok, c_up):
        c.start()
    entry_wait()
    ag_start(0)
    own_wout()
    a2a_start(tokens, tokb, 0)
    ag_start(1)
    a2a_start(upstream, upb, 1)
    ag(0, 0, 0)
    ag(0, 0, 1)
    ag(1, 0, 0)
    ag(0, 1, 0)
    ag(1, 0, 1)
    A2F(0)
    ag(0, 1, 1)
    ag(1, 1, 0)
    A2W(0)
    P_(0, 1, 1)
    ag(1, 1, 1)
    ag(0, 2, 0)
    P_(0, 0, 1)
    A2F(1)
    S_(0, 1)
    ag(0, 2, 1)
    P_(0, 2, 1)
    S_(0, 0)
    ag(1, 2, 0)
    S_(0, 2)
    ag(1, 2, 1)
    A2W(1)
    P_(1, 2, 1)
    S_(1, 2)
    ag(0, 3, 1)
    ag(0, 3, 0)
    P_(0, 3, 1)
    S_(0, 3)
    P_(1, 0, 2)
    ag(1, 3, 0)
    transpose(upT, upb)
    S_(1, 0)
    ag(1, 3, 1)
    P_(1, 3, 1)
    U_(0, 2)
    S_(1, 3)
    U_(1, 2)
    U_(0, 3)
    U_(0, 0)
    S_(1, 1)
    V_(0, 2)
    U_(0, 1)
    U_(1, 3)
    U_(1, 0)
    V_(0, 3)
    V_(1, 2)
    V_(0, 0)
    U_(1, 1)
    GV(0, 2)
    V_(0, 1)
    V_(1, 3)
    V_(1, 0)
    GV(0, 3)
    GV(1, 2)
    V_(1, 1)
    GV(1, 3)
    GU(0, 2)
    transpose(tokT, tokb)
    GV(0, 1)
    grad_mm(0, 2, 1)
    GU(0, 3)
    grad_mm(0, 3, 1)
    RS(0, 0)
    GU(1, 2)
    GV(1, 0)
    GV(0, 0)
    GV(1, 1)
    grad_mm(1, 2, 1)
    GU(1, 3)
    grad_mm(1, 3, 1)
    RS(1, 0)
    transpose(w1T, w1)
    GU(0, 1)
    GU(0, 0)
    RS(0, 1)
    GU(1, 0)
    GU(1, 1)
    TG()
    RS(1, 1)
    grad_mm(1, 1, 1)
    grad_mm(0, 1, 1)
    drain(40)
    RS(0, 2)
    grad_mm(0, 0, 1)
    grad_mm(1, 0, 1)
    drain(40)
    RS(1, 2)
    TG2()
    RS(0, 3)
    drain(40)
    RS(1, 3)
    RS_end(0)
    c_o = pltpu.make_async_copy(res.at[0], outg_out, loc_sem.at[0])
    c_o.start()
    TGE()
    RS_end(1)
    c_i = pltpu.make_async_copy(res.at[1], ing_out, loc_sem.at[2])
    c_i.start()
    drain()
    for n in range(3):
        a2a_wait(n, a2a_send)
    c_o.wait()
    c_i.wait()


def finish(tg, ing, outg, tg_o, ing_o, outg_o, tb, tf, sem):
    NC = 4
    D = tb.shape[1]
    C = D // NC
    c_o = pltpu.make_async_copy(outg, outg_o, sem.at[0])
    c_o.start()
    c_i = pltpu.make_async_copy(ing, ing_o, sem.at[1])
    c_i.start()
    ins = [pltpu.make_async_copy(tg.at[:, pl.ds(C * c, C)], tb.at[:, pl.ds(C * c, C)], sem.at[2 + c]) for c in range(NC)]
    for c in ins:
        c.start()
    outs = []
    for n in range(NC):
        ins[n].wait()
        cols = pl.ds(C * n, C)
        tf[:, cols] = tb[:, cols].astype(F32)
        o = pltpu.make_async_copy(tf.at[:, cols], tg_o.at[:, cols], sem.at[2 + NC + n])
        o.start()
        outs.append(o)
    c_o.wait()
    c_i.wait()
    for o in outs:
        o.wait()


def make(mesh):
    NXL, NDP, NZ = mesh.shape["dcn"], mesh.shape["dp"], mesh.shape["tp"]
    NP = NXL * NDP
    NS = 1
    while NS * NS * 2 < NP:
        NS += 1

    def per_device(tokens, upstream, w_in, w_out):
        T, D = tokens.shape
        B = D // NP
        BC = 2 * B
        H = NZ // 2
        HL = 128 * H
        R = NP * T
        RC = R // 2
        UR = R // NS
        VR = UR // NS
        cfg = (NXL, NDP, NZ, NS, T, B)
        DMA = pltpu.SemaphoreType.DMA
        VM = pltpu.VMEM
        scratch = [
            VM((R, BC), BF16),
            VM((R, BC), BF16),
            VM((BC, R), BF16),
            VM((BC, R), BF16),
            VM((BC, 128), BF16),
            VM((BC, 128), BF16),
            VM((BC, HL), BF16),
            VM((BC, HL), BF16),
            VM((HL, BC), BF16),
            VM((128, BC), BF16),
            VM((2, R, HL), F32),
            VM((2, NS - 1, UR, HL), F32),
            VM((2, UR, HL), F32),
            VM((2, NS - 1, VR, HL), F32),
            VM((VR, HL), F32),
            VM((2, R, HL), BF16),
            VM((2, BC, HL), F32),
            VM((2, B, 128), F32),
            VM((2 * H, BC, 128), BF16),
            VM((2 * H, BC, 128), BF16),
            VM((2, 2, B, 128), BF16),
            VM((R, BC), F32),
            VM((RC, BC), F32),
            VM((RC, BC), BF16),
            VM((2, B, 128), F32),
            DMA((5,)),
            DMA((3,)),
            DMA((3,)),
            DMA((5,)),
            DMA((5,)),
            DMA((8 * H,)),
            DMA((8 * H,)),
            DMA((4 * H,)),
            DMA((4 * H,)),
            DMA((4,)),
            DMA((4,)),
            DMA((4 * H, NS - 1)),
            DMA((4 * H, NS - 1)),
            DMA((4 * H, NS - 1)),
            DMA((4 * H, NS - 1)),
        ]
        tg, ing, outg = pl.pallas_call(
            functools.partial(kernel, cfg),
            out_shape=(
                jax.ShapeDtypeStruct((T, D), BF16),
                jax.ShapeDtypeStruct((B, 128), F32),
                jax.ShapeDtypeStruct((B, 128), F32),
            ),
            in_specs=[pl.BlockSpec(memory_space=pl.ANY)] * 4,
            out_specs=tuple([pl.BlockSpec(memory_space=pl.ANY)] * 3),
            scratch_shapes=scratch,
            compiler_params=pltpu.CompilerParams(
                collective_id=0, has_side_effects=True, vmem_limit_bytes=105 * 2**19
            ),
        )(tokens, upstream, w_in, w_out)
        tg_f, ing_f, outg_f = pl.pallas_call(
            finish,
            out_shape=(
                jax.ShapeDtypeStruct((T, D), F32),
                jax.ShapeDtypeStruct((B, 128), F32),
                jax.ShapeDtypeStruct((B, 128), F32),
            ),
            in_specs=[pl.BlockSpec(memory_space=pl.ANY)] * 3,
            out_specs=tuple([pl.BlockSpec(memory_space=pl.ANY)] * 3),
            scratch_shapes=[
                pltpu.VMEM((T, D), BF16),
                pltpu.VMEM((T, D), F32),
                DMA((10,)),
            ],
            compiler_params=pltpu.CompilerParams(vmem_limit_bytes=50 * 2**20),
        )(tg, ing, outg)
        return tg_f, ing_f, outg_f.T

    return per_device


def solution(mesh):
    placed = (
        P(("dcn", "dp", "tp"), None),
        P(("dcn", "dp", "tp"), None),
        P(None, "tp"),
        P("tp", None),
    )
    return jax.shard_map(
        make(mesh),
        mesh=mesh,
        in_specs=placed,
        out_specs=(P(("dcn", "dp", "tp"), None), P(("dcn", "dp"), "tp"), P("tp", ("dcn", "dp"))),
        check_vma=False,
    )
```

```python
import functools

import jax
import jax.numpy as jnp
from jax import lax
from jax.experimental import pallas as pl
from jax.experimental.pallas import tpu as pltpu
from jax.sharding import PartitionSpec as P

MESH = pl.DeviceIdType.MESH
F32 = jnp.float32
BF16 = jnp.bfloat16


def mult(value, of):
    return pl.multiple_of(value, of)


def kernel(
    cfg,
    tokens, upstream, w_in, w_out,
    tg_out, ing_out, outg_out,
    tokb, upb, tokT, upT, own1, own2, w1, w2, w1T, wo_tmp,
    prep, urecv, usum, vrecv, vv, pos, posv, gath,
    grad, ownp, zsend, zrecv, zfin, tgp, tgx, tgb,
    loc_sem, a2a_send, a2a_recv, f_send, f_recv, ag_sent, ag_recv, rs_sent, rs_recv,
    fin_recv, u_send, u_recv, v_send, v_recv,
):
    NXL, NDP, NZ, NS, T, B = cfg
    NP = NXL * NDP
    NC = NP // 2
    H = NZ // 2
    BC = 2 * B
    R = NP * T
    RC = R // 2
    UR = R // NS
    VR = UR // NS
    HP = B // 2

    z = lax.axis_index("tp")
    dcn = lax.axis_index("dcn")
    dp = lax.axis_index("dp")
    k = dp % 2
    y = (dp // 2) % NS
    x = (dp // (2 * NS)) * NXL + dcn
    p = (dcn * NDP + dp) // 2
    u = jnp.where(k == 0, x, y)
    v = jnp.where(k == 0, y, x)
    up = (z + 1) % NZ
    down = (z + NZ - 1) % NZ

    def dev(x_, y_, k_):
        return (x_ % NXL, (x_ // NXL) * (2 * NS) + y_ * 2 + k_, z)

    def chip(p_):
        i_ = 2 * p_ + k
        return (i_ // NDP, i_ % NDP, z)

    def at_z(z_, k_):
        return (dcn, dp - k + k_, z_)

    sib = dev(x, y, 1 - k)

    def u_peer(u_):
        return dev(jnp.where(k == 0, u_, x), jnp.where(k == 0, y, u_), k)

    def v_peer(v_):
        return dev(jnp.where(k == 0, x, v_), jnp.where(k == 0, v_, y), k)

    ag_z = jnp.where(k == 0, up, down)
    rs_z = jnp.where(k == 0, down, up)

    sends = []

    def send(src, dst, ss, rs, to, when=None):
        c = pltpu.make_async_remote_copy(
            src_ref=src, dst_ref=dst, send_sem=ss, recv_sem=rs, device_id=to, device_id_type=MESH
        )
        if when is None:
            c.start()
        else:
            pl.when(when)(c.start)
        sends.append((when, c))
        return c

    def landed(ref, sem):
        pltpu.make_async_copy(ref, ref, sem).wait()

    def drain(keep=0):
        while len(sends) > keep:
            when, c = sends.pop(0)
            if when is None:
                c.wait_send()
            else:
                pl.when(when)(c.wait_send)

    LAST = H - 1

    def lanes(c, n=1):
        return pl.ds(128 * c, 128 * n)

    barrier = pltpu.get_barrier_semaphore()
    cols = pl.ds(mult(BC * p, 128), BC)
    my_tok = pl.ds(mult(RC * k + T * p, T), T)
    my_half = pl.ds(mult(RC * k, RC), RC)
    sib_half = pl.ds(mult(RC * (1 - k), RC), RC)

    def entry():
        for z_ in (up, down) if NZ > 2 else (up,):
            for k_ in (0, 1):
                pl.semaphore_signal(barrier, inc=1, device_id=at_z(z_, k_), device_id_type=MESH)
        pl.semaphore_signal(barrier, inc=1, device_id=sib, device_id_type=MESH)

        @pl.loop(1, NC)
        def _(d):
            pl.semaphore_signal(barrier, inc=1, device_id=chip((p + d) % NC), device_id_type=MESH)

    c_win = pltpu.make_async_copy(w_in.at[pl.ds(mult(BC * p, 128), BC), :], own1, loc_sem.at[0])
    c_wout = pltpu.make_async_copy(w_out.at[:, cols], wo_tmp, loc_sem.at[1])
    c_tok = pltpu.make_async_copy(tokens.at[:, cols], tokb.at[my_tok, :], loc_sem.at[2])
    c_up = pltpu.make_async_copy(upstream.at[:, cols], upb.at[my_tok, :], loc_sem.at[3])

    def entry_wait():
        pl.semaphore_wait(barrier, NC + (4 if NZ > 2 else 2))

    def own_wout():
        c_win.wait()
        c_wout.wait()
        own2[...] = wo_tmp[...].T

        @pl.when(k == 0)
        def _():
            w1[:, lanes(LAST)] = own1[...]
            w2[:, lanes(LAST)] = own2[...]

    def rows_at(q):
        return pl.ds(HP * q, HP)

    def ag_block(wi, step):
        return (own1, own2)[wi] if step == 0 else (w1, w2)[wi].at[:, lanes(step - 1)]

    def ag_sem(wi, step, q):
        return (wi * H + step) * 4 + q

    def ag_send(wi, step, q):
        w = (w1, w2)[wi]
        n = ag_sem(wi, step, q)
        if wi == 0 and step == 0:
            src = w_in.at[pl.ds(mult(BC * p + HP * q, 32), HP), :]
        else:
            src = ag_block(wi, step).at[rows_at(q), :]
        if step < H - 1:
            send(src, w.at[rows_at(q), lanes(step)], ag_sent.at[n], ag_recv.at[n], at_z(ag_z, k))
        else:
            send(
                src, w.at[rows_at(q), lanes(LAST)], ag_sent.at[n], ag_recv.at[n], at_z(ag_z, 1),
                when=k == q // 2,
            )


    def ag_start(wi):
        for q in range(4):
            ag_send(wi, 0, q)

    def ag(wi, step, half):
        w = (w1, w2)[wi]
        for q in (2 * half, 2 * half + 1):
            arrived = w.at[rows_at(q), lanes(step)]
            if step < H - 1:
                landed(arrived, ag_recv.at[ag_sem(wi, step, q)])
                ag_send(wi, step + 1, q)
            else:
                pl.when(k == 1)(functools.partial(landed, arrived, ag_recv.at[ag_sem(wi, step, q)]))

    def a2a_start(src, dst, n):
        @pl.loop(1, NC)
        def _(d):
            to = (p + d) % NC
            pltpu.make_async_remote_copy(
                src_ref=src.at[:, pl.ds(mult(BC * to, 128), BC)],
                dst_ref=dst.at[my_tok, :],
                send_sem=a2a_send.at[n],
                recv_sem=a2a_recv.at[n],
                device_id=chip(to),
                device_id_type=MESH,
            ).start()

    def a2a_wait(n, sems):
        landed(tokb.at[pl.ds(0, RC - T), :], sems.at[n])

    def A2F(n):
        (c_tok, c_up)[n].wait()
        a2a_wait(n, a2a_recv)
        ref = (tokb, upb)[n].at[my_half, :]
        send(ref, ref, f_send.at[n], f_recv.at[n], sib)

    def A2W(n):
        landed((tokb, upb)[n].at[sib_half, :], f_recv.at[n])

    mine = pl.ds(mult(UR * u + VR * v, VR), VR)
    u_rows = pl.ds(mult(UR * u, UR), UR)
    pend = {}

    def P_(n, c, count):
        lhs, w = ((tokb, w1), (upb, w2))[n]
        prep[n, :, lanes(c, count)] = jnp.dot(lhs[...], w[:, lanes(c, count)], preferred_element_type=F32)

    def S_(n, c):
        q = n * H + c
        out = []
        for r in [2, 1, 3] if NS == 4 else range(1, NS):
            uu = (u + r) % NS
            out.append(
                send(
                    prep.at[n, pl.ds(mult(UR * uu, UR), UR), lanes(c)], urecv.at[n, r - 1, :, lanes(c)],
                    u_send.at[q, r - 1], u_recv.at[q, r - 1], u_peer(uu),
                )
            )
        pend["u", n, c] = out

    def U_(n, c):
        q = n * H + c
        for d in pend["u", n, c]:
            d.wait_recv()
        tot = prep[n, u_rows, lanes(c)]
        for r in range(NS - 1):
            tot = tot + urecv[n, r, :, lanes(c)]
        usum[n, :, lanes(c)] = tot
        if c == -1:
            vv[n, v] = tot
            mine_all = usum.at[n, :, lanes(c)]
            pend["v", n, c] = [
                send(mine_all, vv.at[n, v], v_send.at[q, r - 1], v_recv.at[q, r - 1], v_peer((v + r) % NS))
                for r in range(1, NS)
            ]
            return
        pend["v", n, c] = [
            send(
                usum.at[n, pl.ds(mult(VR * ((v + r) % NS), VR), VR), lanes(c)], vrecv.at[n, r - 1, :, lanes(c)],
                v_send.at[q, r - 1], v_recv.at[q, r - 1], v_peer((v + r) % NS),
            )
            for r in range(1, NS)
        ]

    def V_(n, c):
        q = 2 * H + n * H + c
        for d in pend["v", n, c]:
            d.wait_recv()
        if c == -1:
            tot = vv[n, 0]
            for r in range(1, NS):
                tot = tot + vv[n, r]
            if n == 0:
                positive = jnp.maximum(tot, 0.0)
                posv[...] = positive
                gath[0, u_rows, lanes(c)] = (positive * positive).astype(BF16)
            else:
                gath[1, u_rows, lanes(c)] = (tot * 2.0 * posv[...]).astype(BF16)
            return
        tot = usum[n, pl.ds(mult(VR * v, VR), VR), lanes(c)]
        for r in range(NS - 1):
            tot = tot + vrecv[n, r, :, lanes(c)]
        if n == 0:
            positive = jnp.maximum(tot, 0.0)
            pos[:, lanes(c)] = positive
            gath[0, mine, lanes(c)] = (positive * positive).astype(BF16)
        else:
            gath[1, mine, lanes(c)] = (tot * 2.0 * pos[:, lanes(c)]).astype(BF16)
        ref = gath.at[n, mine, lanes(c)]
        pend["gv", n, c] = [
            send(ref, ref, v_send.at[q, r - 1], v_recv.at[q, r - 1], v_peer((v + r) % NS)) for r in range(1, NS)
        ]

    def GV(n, c):
        q = 2 * H + n * H + c
        if c != -1:
            for d in pend["gv", n, c]:
                d.wait_recv()
        ref = gath.at[n, u_rows, lanes(c)]
        pend["gu", n, c] = [
            send(ref, ref, u_send.at[q, r - 1], u_recv.at[q, r - 1], u_peer((u + r) % NS)) for r in range(1, NS)
        ]

    def GU(n, c):
        for d in pend["gu", n, c]:
            d.wait_recv()

    def grad_mm(n, c, count):
        lhsT = (upT, tokT)[n]
        grad[n, :, lanes(c, count)] = jnp.dot(lhsT[...], gath[n, :, lanes(c, count)], preferred_element_type=F32)

    def half_rows(hf):
        return pl.ds(mult(B * hf, 64), B)

    def rs_one(n, step, hf, recv):
        q = n * H + step
        for m in (0, 1):
            rows = pl.ds(mult(B * hf + HP * m, 32), HP)
            val = grad[n, rows, lanes(H - 1 - step)]
            if recv:
                landed(zrecv.at[q - 1, rows, :], rs_recv.at[4 * (q - 1) + 2 * hf + m])
                val = val + zrecv[q - 1, rows, :].astype(F32)
            zsend[q, rows, :] = val.astype(BF16)
            src = zsend.at[q, rows, :]
            s = 4 * q + 2 * hf + m
            if step < H - 1:
                send(src, zrecv.at[q, rows, :], rs_sent.at[s], rs_recv.at[s], at_z(rs_z, k))
            else:
                dst = zfin.at[n, k, pl.ds(HP * m, HP), :]
                send(src, dst, rs_sent.at[s], fin_recv.at[4 * n + 2 * k + m], at_z(rs_z, hf))

    def RS(n, step):
        if step == 0:
            q = n * H

            @pl.when(k == 1)
            def _():
                zsend[q] = grad[n, :, lanes(LAST)].astype(BF16)

            for hf, to in ((0, at_z(up, 1)), (1, at_z(down, 0))):
                for m in (0, 1):
                    rows = pl.ds(B * hf + HP * m, HP)
                    s = 4 * q + 2 * hf + m
                    send(
                        zsend.at[q, rows, :], zrecv.at[q, rows, :], rs_sent.at[s], rs_recv.at[s], to, when=k == 1
                    )
            rs_one(n, 1, k, False)
            send(
                grad.at[n, pl.ds(B, B), lanes(LAST)], ownp.at[n], f_send.at[2 + n], f_recv.at[2 + n], sib, when=k == 0
            )
        elif step == 1:
            rs_one(n, 1, 1 - k, True)
        else:
            rs_one(n, step, k, True)
            rs_one(n, step, 1 - k, True)

    def RS_end(n):
        for d in (0, 1):
            for m in (0, 1):
                landed(zfin.at[n, d, pl.ds(HP * m, HP), :], fin_recv.at[4 * n + 2 * d + m])
        tot = zfin[n, 0].astype(F32) + zfin[n, 1].astype(F32)

        @pl.when(k == 0)
        def _():
            (outg_out, ing_out)[n][...] = tot + grad[n, 0:B, lanes(LAST)]

        @pl.when(k == 1)
        def _():
            landed(ownp.at[n], f_recv.at[2 + n])
            (outg_out, ing_out)[n][...] = tot + ownp[n]

    TR = min(128, RC)

    def tg_mm(half):
        @pl.loop(0, RC // TR)
        def _(t):
            rows = pl.ds(mult(RC * half + TR * t, TR), TR)
            tgp[rows, :] = jnp.dot(gath[1, rows, :], w1T[...], preferred_element_type=F32)

    def TG():
        tg_mm(1 - k)
        send(tgp.at[sib_half, :], tgx, f_send.at[4], f_recv.at[4], sib)
        tg_mm(k)

    c_t = pltpu.make_async_copy(tgb.at[pl.ds(mult(T * p, T), T), :], tg_out.at[:, cols], loc_sem.at[4])

    def TG2():
        landed(tgx, f_recv.at[4])

        @pl.loop(0, RC // TR)
        def _(t):
            rows = pl.ds(mult(TR * t, TR), TR)
            tgb[rows, :] = (tgp[pl.ds(mult(RC * k + TR * t, TR), TR), :] + tgx[rows, :]).astype(BF16)

        @pl.loop(1, NC)
        def _(d):
            to = (p + d) % NC
            pltpu.make_async_remote_copy(
                src_ref=tgb.at[pl.ds(mult(T * to, T), T), :],
                dst_ref=tg_out.at[:, cols],
                send_sem=a2a_send.at[2],
                recv_sem=a2a_recv.at[2],
                device_id=chip(to),
                device_id_type=MESH,
            ).start()

        c_t.start()

    def TGE():
        landed(tg_out.at[:, pl.ds(0, BC * (NC - 1))], a2a_recv.at[2])
        c_t.wait()

    def transpose(dst, src):
        dst[...] = src[...].T

    entry()
    for c in (c_win, c_wout, c_tok, c_up):
        c.start()
    entry_wait()
    ag_start(0)
    a2a_start(tokens, tokb, 0)
    ag(0, 0, 0)
    ag(0, 0, 1)
    a2a_start(upstream, upb, 1)
    ag(0, 1, 0)
    own_wout()
    ag(0, 1, 1)
    A2F(0)
    ag_start(1)
    A2W(0)
    P_(0, 0, 1)
    S_(0, 0)
    ag(0, 2, 0)
    ag(0, 2, 1)
    P_(0, 2, 1)
    S_(0, 2)
    P_(0, 1, 1)
    S_(0, 1)
    ag(1, 0, 0)
    A2F(1)
    ag(1, 0, 1)
    ag(0, 3, 1)
    ag(0, 3, 0)
    P_(0, 3, 1)
    S_(0, 3)
    ag(1, 1, 0)
    U_(0, 2)
    A2W(1)
    U_(0, 0)
    P_(1, 0, 1)
    ag(1, 1, 1)
    S_(1, 0)
    P_(1, 1, 1)
    U_(0, 1)
    transpose(w1T, w1)
    ag(1, 2, 0)
    U_(0, 3)
    V_(0, 2)
    S_(1, 1)
    ag(1, 2, 1)
    P_(1, 2, 1)
    S_(1, 2)
    V_(0, 1)
    transpose(upT, upb)
    V_(0, 3)
    GV(0, 2)
    V_(0, 0)
    U_(1, 0)
    ag(1, 3, 0)
    ag(1, 3, 1)
    P_(1, 3, 1)
    S_(1, 3)
    U_(1, 2)
    GV(0, 3)
    GV(0, 0)
    GU(0, 2)
    U_(1, 1)
    V_(1, 0)
    U_(1, 3)
    GV(0, 1)
    grad_mm(0, 2, 1)
    V_(1, 2)
    GU(0, 3)
    grad_mm(0, 3, 1)
    RS(0, 0)
    V_(1, 1)
    V_(1, 3)
    GU(0, 1)
    transpose(tokT, tokb)
    GV(1, 0)
    GV(1, 2)
    RS(0, 1)
    GU(0, 0)
    GV(1, 1)
    grad_mm(0, 1, 1)
    GV(1, 3)
    drain(40)
    RS(0, 2)
    GU(1, 2)
    GU(1, 1)
    GU(1, 0)
    grad_mm(1, 2, 1)
    GU(1, 3)
    grad_mm(1, 3, 1)
    RS(1, 0)
    grad_mm(1, 0, 2)
    TG()
    RS(1, 1)
    grad_mm(0, 0, 1)
    RS(0, 3)
    TG2()
    drain(40)
    RS(1, 2)
    RS_end(0)
    drain(40)
    RS(1, 3)
    TGE()
    RS_end(1)
    drain()
    for n in range(3):
        a2a_wait(n, a2a_send)


def finish(tg, ing, outg, tg_o, ing_o, outg_o, tf, sem):
    NC = 4
    D = tg.shape[1]
    C = D // NC
    c_o = pltpu.make_async_copy(outg, outg_o, sem.at[0])
    c_o.start()
    c_i = pltpu.make_async_copy(ing, ing_o, sem.at[1])
    c_i.start()
    outs = []
    for n in range(NC):
        cols = pl.ds(C * n, C)
        tf[:, cols] = tg[:, cols].astype(F32)
        o = pltpu.make_async_copy(tf.at[:, cols], tg_o.at[:, cols], sem.at[2 + NC + n])
        o.start()
        outs.append(o)
    c_o.wait()
    c_i.wait()
    for o in outs:
        o.wait()


def make(mesh):
    NXL, NDP, NZ = mesh.shape["dcn"], mesh.shape["dp"], mesh.shape["tp"]
    NP = NXL * NDP
    NS = 1
    while NS * NS * 2 < NP:
        NS += 1

    def per_device(tokens, upstream, w_in, w_out):
        T, D = tokens.shape
        B = D // NP
        BC = 2 * B
        H = NZ // 2
        HL = 128 * H
        R = NP * T
        RC = R // 2
        UR = R // NS
        VR = UR // NS
        cfg = (NXL, NDP, NZ, NS, T, B)
        DMA = pltpu.SemaphoreType.DMA
        VM = pltpu.VMEM
        scratch = [
            VM((R, BC), BF16),
            VM((R, BC), BF16),
            VM((BC, R), BF16),
            VM((BC, R), BF16),
            VM((BC, 128), BF16),
            VM((BC, 128), BF16),
            VM((BC, HL), BF16),
            VM((BC, HL), BF16),
            VM((HL, BC), BF16),
            VM((128, BC), BF16),
            VM((2, R, HL), F32),
            VM((2, NS - 1, UR, HL), F32),
            VM((2, UR, HL), F32),
            VM((2, NS - 1, VR, HL), F32),
            VM((2, NS, UR, 128), F32),
            VM((VR, HL), F32),
            VM((UR, 128), F32),
            VM((2, R, HL), BF16),
            VM((2, BC, HL), F32),
            VM((2, B, 128), F32),
            VM((2 * H, BC, 128), BF16),
            VM((2 * H, BC, 128), BF16),
            VM((2, 2, B, 128), BF16),
            VM((R, BC), F32),
            VM((RC, BC), F32),
            VM((RC, BC), BF16),
            DMA((5,)),
            DMA((3,)),
            DMA((3,)),
            DMA((5,)),
            DMA((5,)),
            DMA((8 * H,)),
            DMA((8 * H,)),
            DMA((8 * H,)),
            DMA((8 * H,)),
            DMA((8,)),
            DMA((4 * H, NS - 1)),
            DMA((4 * H, NS - 1)),
            DMA((4 * H, NS - 1)),
            DMA((4 * H, NS - 1)),
        ]
        tg, ing, outg = pl.pallas_call(
            functools.partial(kernel, cfg),
            out_shape=(
                jax.ShapeDtypeStruct((T, D), BF16),
                jax.ShapeDtypeStruct((B, 128), F32),
                jax.ShapeDtypeStruct((B, 128), F32),
            ),
            in_specs=[pl.BlockSpec(memory_space=pl.ANY)] * 4,
            out_specs=(
                pl.BlockSpec(memory_space=pl.ANY),
                pl.BlockSpec(memory_space=pltpu.VMEM),
                pl.BlockSpec(memory_space=pltpu.VMEM),
            ),
            scratch_shapes=scratch,
            compiler_params=pltpu.CompilerParams(
                collective_id=0, has_side_effects=True, vmem_limit_bytes=105 * 2**19
            ),
        )(tokens, upstream, w_in, w_out)
        tg_f, ing_f, outg_f = pl.pallas_call(
            finish,
            out_shape=(
                jax.ShapeDtypeStruct((T, D), F32),
                jax.ShapeDtypeStruct((B, 128), F32),
                jax.ShapeDtypeStruct((B, 128), F32),
            ),
            in_specs=[pl.BlockSpec(memory_space=pltpu.VMEM)] * 3,
            out_specs=tuple([pl.BlockSpec(memory_space=pl.ANY)] * 3),
            scratch_shapes=[
                pltpu.VMEM((T, D), F32),
                DMA((10,)),
            ],
            compiler_params=pltpu.CompilerParams(vmem_limit_bytes=50 * 2**20),
        )(tg, ing, outg)
        return tg_f, ing_f, outg_f.T

    return per_device


def solution(mesh):
    placed = (
        P(("dcn", "dp", "tp"), None),
        P(("dcn", "dp", "tp"), None),
        P(None, "tp"),
        P("tp", None),
    )
    return jax.shard_map(
        make(mesh),
        mesh=mesh,
        in_specs=placed,
        out_specs=(P(("dcn", "dp", "tp"), None), P(("dcn", "dp"), "tp"), P("tp", ("dcn", "dp"))),
        check_vma=False,
    )
```

```python
import functools

import jax
import jax.numpy as jnp
from jax import lax
from jax.experimental import pallas as pl
from jax.experimental.pallas import tpu as pltpu
from jax.sharding import PartitionSpec as P

MESH = pl.DeviceIdType.MESH
F32 = jnp.float32
BF16 = jnp.bfloat16


def mult(value, of):
    return pl.multiple_of(value, of)


def kernel(
    cfg,
    tokens, upstream, w_in, w_out,
    tg_out, ing_out, outg_out,
    tokb, upb, tokT, upT, own1, own2, w1, w2, w1T, wo_tmp,
    prep, urecv, usum, vrecv, vv, pos, posv, gath,
    grad, ownp, zsend, zrecv, zfin, tgp, tgx, tgb,
    loc_sem, a2a_send, a2a_recv, f_send, f_recv, ag_sent, ag_recv, rs_sent, rs_recv,
    fin_recv, u_send, u_recv, v_send, v_recv,
):
    NXL, NDP, NZ, NS, T, B = cfg
    NP = NXL * NDP
    NC = NP // 2
    H = NZ // 2
    BC = 2 * B
    R = NP * T
    RC = R // 2
    UR = R // NS
    VR = UR // NS
    HP = B // 2

    z = lax.axis_index("tp")
    dcn = lax.axis_index("dcn")
    dp = lax.axis_index("dp")
    k = dp % 2
    y = (dp // 2) % NS
    x = (dp // (2 * NS)) * NXL + dcn
    p = (dcn * NDP + dp) // 2
    u = jnp.where(k == 0, x, y)
    v = jnp.where(k == 0, y, x)
    up = (z + 1) % NZ
    down = (z + NZ - 1) % NZ

    def dev(x_, y_, k_):
        return (x_ % NXL, (x_ // NXL) * (2 * NS) + y_ * 2 + k_, z)

    def chip(p_):
        i_ = 2 * p_ + k
        return (i_ // NDP, i_ % NDP, z)

    def at_z(z_, k_):
        return (dcn, dp - k + k_, z_)

    sib = dev(x, y, 1 - k)

    def u_peer(u_):
        return dev(jnp.where(k == 0, u_, x), jnp.where(k == 0, y, u_), k)

    def v_peer(v_):
        return dev(jnp.where(k == 0, x, v_), jnp.where(k == 0, v_, y), k)

    ag_z = jnp.where(k == 0, up, down)
    rs_z = jnp.where(k == 0, down, up)

    sends = []

    def send(src, dst, ss, rs, to, when=None):
        c = pltpu.make_async_remote_copy(
            src_ref=src, dst_ref=dst, send_sem=ss, recv_sem=rs, device_id=to, device_id_type=MESH
        )
        if when is None:
            c.start()
        else:
            pl.when(when)(c.start)
        sends.append((when, c))
        return c

    def landed(ref, sem):
        pltpu.make_async_copy(ref, ref, sem).wait()

    def drain(keep=0):
        while len(sends) > keep:
            when, c = sends.pop(0)
            if when is None:
                c.wait_send()
            else:
                pl.when(when)(c.wait_send)

    LAST = H - 1

    def lanes(c, n=1):
        return pl.ds(128 * c, 128 * n)

    barrier = pltpu.get_barrier_semaphore()
    cols = pl.ds(mult(BC * p, 128), BC)
    my_tok = pl.ds(mult(RC * k + T * p, T), T)
    my_half = pl.ds(mult(RC * k, RC), RC)
    sib_half = pl.ds(mult(RC * (1 - k), RC), RC)

    def entry():
        for z_ in (up, down) if NZ > 2 else (up,):
            for k_ in (0, 1):
                pl.semaphore_signal(barrier, inc=1, device_id=at_z(z_, k_), device_id_type=MESH)
        pl.semaphore_signal(barrier, inc=1, device_id=sib, device_id_type=MESH)

        @pl.loop(1, NC)
        def _(d):
            pl.semaphore_signal(barrier, inc=1, device_id=chip((p + d) % NC), device_id_type=MESH)

    c_win = pltpu.make_async_copy(w_in.at[pl.ds(mult(BC * p, 128), BC), :], own1, loc_sem.at[0])
    c_wout = pltpu.make_async_copy(w_out.at[:, cols], wo_tmp, loc_sem.at[1])
    c_tok = pltpu.make_async_copy(tokens.at[:, cols], tokb.at[my_tok, :], loc_sem.at[2])
    c_up = pltpu.make_async_copy(upstream.at[:, cols], upb.at[my_tok, :], loc_sem.at[3])

    def entry_wait():
        pl.semaphore_wait(barrier, NC + (4 if NZ > 2 else 2))

    def own_wout():
        c_win.wait()
        c_wout.wait()
        own2[...] = wo_tmp[...].T

        @pl.when(k == 0)
        def _():
            w1[:, lanes(LAST)] = own1[...]
            w2[:, lanes(LAST)] = own2[...]

    def rows_at(q):
        return pl.ds(HP * q, HP)

    def ag_block(wi, step):
        return (own1, own2)[wi] if step == 0 else (w1, w2)[wi].at[:, lanes(step - 1)]

    def ag_sem(wi, step, q):
        return (wi * H + step) * 4 + q

    def ag_send(wi, step, q):
        w = (w1, w2)[wi]
        n = ag_sem(wi, step, q)
        if wi == 0 and step == 0:
            src = w_in.at[pl.ds(mult(BC * p + HP * q, 32), HP), :]
        else:
            src = ag_block(wi, step).at[rows_at(q), :]
        if step < H - 1:
            send(src, w.at[rows_at(q), lanes(step)], ag_sent.at[n], ag_recv.at[n], at_z(ag_z, k))
        else:
            send(
                src, w.at[rows_at(q), lanes(LAST)], ag_sent.at[n], ag_recv.at[n], at_z(ag_z, 1),
                when=k == q // 2,
            )


    def ag_start(wi):
        for q in range(4):
            ag_send(wi, 0, q)

    def ag(wi, step, half):
        w = (w1, w2)[wi]
        for q in (2 * half, 2 * half + 1):
            arrived = w.at[rows_at(q), lanes(step)]
            if step < H - 1:
                landed(arrived, ag_recv.at[ag_sem(wi, step, q)])
                ag_send(wi, step + 1, q)
            else:
                pl.when(k == 1)(functools.partial(landed, arrived, ag_recv.at[ag_sem(wi, step, q)]))

    def a2a_start(src, dst, n):
        @pl.loop(1, NC)
        def _(d):
            to = (p + d) % NC
            pltpu.make_async_remote_copy(
                src_ref=src.at[:, pl.ds(mult(BC * to, 128), BC)],
                dst_ref=dst.at[my_tok, :],
                send_sem=a2a_send.at[n],
                recv_sem=a2a_recv.at[n],
                device_id=chip(to),
                device_id_type=MESH,
            ).start()

    def a2a_wait(n, sems):
        landed(tokb.at[pl.ds(0, RC - T), :], sems.at[n])

    def A2F(n):
        (c_tok, c_up)[n].wait()
        a2a_wait(n, a2a_recv)
        ref = (tokb, upb)[n].at[my_half, :]
        send(ref, ref, f_send.at[n], f_recv.at[n], sib)

    def A2W(n):
        landed((tokb, upb)[n].at[sib_half, :], f_recv.at[n])

    mine = pl.ds(mult(UR * u + VR * v, VR), VR)
    u_rows = pl.ds(mult(UR * u, UR), UR)
    pend = {}

    def P_(n, c, count):
        lhs, w = ((tokb, w1), (upb, w2))[n]
        prep[n, :, lanes(c, count)] = jnp.dot(lhs[...], w[:, lanes(c, count)], preferred_element_type=F32)

    def S_(n, c):
        q = n * H + c
        out = []
        for r in [2, 1, 3] if NS == 4 else range(1, NS):
            uu = (u + r) % NS
            out.append(
                send(
                    prep.at[n, pl.ds(mult(UR * uu, UR), UR), lanes(c)], urecv.at[n, r - 1, :, lanes(c)],
                    u_send.at[q, r - 1], u_recv.at[q, r - 1], u_peer(uu),
                )
            )
        pend["u", n, c] = out

    def U_(n, c):
        q = n * H + c
        for d in pend["u", n, c]:
            d.wait_recv()
        tot = prep[n, u_rows, lanes(c)]
        for r in range(NS - 1):
            tot = tot + urecv[n, r, :, lanes(c)]
        usum[n, :, lanes(c)] = tot
        if c == -1:
            vv[n, v] = tot
            mine_all = usum.at[n, :, lanes(c)]
            pend["v", n, c] = [
                send(mine_all, vv.at[n, v], v_send.at[q, r - 1], v_recv.at[q, r - 1], v_peer((v + r) % NS))
                for r in range(1, NS)
            ]
            return
        pend["v", n, c] = [
            send(
                usum.at[n, pl.ds(mult(VR * ((v + r) % NS), VR), VR), lanes(c)], vrecv.at[n, r - 1, :, lanes(c)],
                v_send.at[q, r - 1], v_recv.at[q, r - 1], v_peer((v + r) % NS),
            )
            for r in range(1, NS)
        ]

    def V_(n, c):
        q = 2 * H + n * H + c
        for d in pend["v", n, c]:
            d.wait_recv()
        if c == -1:
            tot = vv[n, 0]
            for r in range(1, NS):
                tot = tot + vv[n, r]
            if n == 0:
                positive = jnp.maximum(tot, 0.0)
                posv[...] = positive
                gath[0, u_rows, lanes(c)] = (positive * positive).astype(BF16)
            else:
                gath[1, u_rows, lanes(c)] = (tot * 2.0 * posv[...]).astype(BF16)
            return
        tot = usum[n, pl.ds(mult(VR * v, VR), VR), lanes(c)]
        for r in range(NS - 1):
            tot = tot + vrecv[n, r, :, lanes(c)]
        if n == 0:
            positive = jnp.maximum(tot, 0.0)
            pos[:, lanes(c)] = positive
            gath[0, mine, lanes(c)] = (positive * positive).astype(BF16)
        else:
            gath[1, mine, lanes(c)] = (tot * 2.0 * pos[:, lanes(c)]).astype(BF16)
        ref = gath.at[n, mine, lanes(c)]
        pend["gv", n, c] = [
            send(ref, ref, v_send.at[q, r - 1], v_recv.at[q, r - 1], v_peer((v + r) % NS)) for r in range(1, NS)
        ]

    def GV(n, c):
        q = 2 * H + n * H + c
        if c != -1:
            for d in pend["gv", n, c]:
                d.wait_recv()
        ref = gath.at[n, u_rows, lanes(c)]
        pend["gu", n, c] = [
            send(ref, ref, u_send.at[q, r - 1], u_recv.at[q, r - 1], u_peer((u + r) % NS)) for r in range(1, NS)
        ]

    def GU(n, c):
        for d in pend["gu", n, c]:
            d.wait_recv()

    def grad_mm(n, c, count):
        lhsT = (upT, tokT)[n]
        grad[n, :, lanes(c, count)] = jnp.dot(lhsT[...], gath[n, :, lanes(c, count)], preferred_element_type=F32)

    def half_rows(hf):
        return pl.ds(mult(B * hf, 64), B)

    def rs_one(n, step, hf, recv):
        q = n * H + step
        for m in (0, 1):
            rows = pl.ds(mult(B * hf + HP * m, 32), HP)
            val = grad[n, rows, lanes(H - 1 - step)]
            if recv:
                landed(zrecv.at[q - 1, rows, :], rs_recv.at[4 * (q - 1) + 2 * hf + m])
                val = val + zrecv[q - 1, rows, :].astype(F32)
            zsend[q, rows, :] = val.astype(BF16)
            src = zsend.at[q, rows, :]
            s = 4 * q + 2 * hf + m
            if step < H - 1:
                send(src, zrecv.at[q, rows, :], rs_sent.at[s], rs_recv.at[s], at_z(rs_z, k))
            else:
                dst = zfin.at[n, k, pl.ds(HP * m, HP), :]
                send(src, dst, rs_sent.at[s], fin_recv.at[4 * n + 2 * k + m], at_z(rs_z, hf))

    def RS(n, step):
        if step == 0:
            q = n * H

            @pl.when(k == 1)
            def _():
                zsend[q] = grad[n, :, lanes(LAST)].astype(BF16)

            for hf, to in ((0, at_z(up, 1)), (1, at_z(down, 0))):
                for m in (0, 1):
                    rows = pl.ds(B * hf + HP * m, HP)
                    s = 4 * q + 2 * hf + m
                    send(
                        zsend.at[q, rows, :], zrecv.at[q, rows, :], rs_sent.at[s], rs_recv.at[s], to, when=k == 1
                    )
            rs_one(n, 1, k, False)
            send(
                grad.at[n, pl.ds(B, B), lanes(LAST)], ownp.at[n], f_send.at[2 + n], f_recv.at[2 + n], sib, when=k == 0
            )
        elif step == 1:
            rs_one(n, 1, 1 - k, True)
        else:
            rs_one(n, step, k, True)
            rs_one(n, step, 1 - k, True)

    def RS_end(n):
        for d in (0, 1):
            for m in (0, 1):
                landed(zfin.at[n, d, pl.ds(HP * m, HP), :], fin_recv.at[4 * n + 2 * d + m])
        tot = zfin[n, 0].astype(F32) + zfin[n, 1].astype(F32)

        @pl.when(k == 0)
        def _():
            (outg_out, ing_out)[n][...] = tot + grad[n, 0:B, lanes(LAST)]

        @pl.when(k == 1)
        def _():
            landed(ownp.at[n], f_recv.at[2 + n])
            (outg_out, ing_out)[n][...] = tot + ownp[n]

    TR = min(128, RC)

    def tg_mm(half):
        @pl.loop(0, RC // TR)
        def _(t):
            rows = pl.ds(mult(RC * half + TR * t, TR), TR)
            tgp[rows, :] = jnp.dot(gath[1, rows, :], w1T[...], preferred_element_type=F32)

    def TG():
        tg_mm(1 - k)
        send(tgp.at[sib_half, :], tgx, f_send.at[4], f_recv.at[4], sib)
        tg_mm(k)

    c_t = pltpu.make_async_copy(tgb.at[pl.ds(mult(T * p, T), T), :], tg_out.at[:, cols], loc_sem.at[4])

    def TG2():
        landed(tgx, f_recv.at[4])

        @pl.loop(0, RC // TR)
        def _(t):
            rows = pl.ds(mult(TR * t, TR), TR)
            tgb[rows, :] = (tgp[pl.ds(mult(RC * k + TR * t, TR), TR), :] + tgx[rows, :]).astype(BF16)

        @pl.loop(1, NC)
        def _(d):
            to = (p + d) % NC
            pltpu.make_async_remote_copy(
                src_ref=tgb.at[pl.ds(mult(T * to, T), T), :],
                dst_ref=tg_out.at[:, cols],
                send_sem=a2a_send.at[2],
                recv_sem=a2a_recv.at[2],
                device_id=chip(to),
                device_id_type=MESH,
            ).start()

        c_t.start()

    def TGE():
        landed(tg_out.at[:, pl.ds(0, BC * (NC - 1))], a2a_recv.at[2])
        c_t.wait()

    def transpose(dst, src):
        dst[...] = src[...].T

    entry()
    for c in (c_win, c_wout, c_tok, c_up):
        c.start()
    entry_wait()
    ag_start(0)
    a2a_start(tokens, tokb, 0)
    ag(0, 0, 0)
    ag(0, 0, 1)
    a2a_start(upstream, upb, 1)
    ag(0, 1, 0)
    own_wout()
    ag(0, 1, 1)
    A2F(0)
    ag_start(1)
    A2W(0)
    P_(0, 0, 1)
    S_(0, 0)
    ag(0, 2, 0)
    ag(0, 2, 1)
    P_(0, 2, 1)
    S_(0, 2)
    P_(0, 1, 1)
    S_(0, 1)
    ag(1, 0, 0)
    A2F(1)
    ag(1, 0, 1)
    ag(0, 3, 1)
    ag(0, 3, 0)
    P_(0, 3, 1)
    S_(0, 3)
    ag(1, 1, 0)
    U_(0, 2)
    A2W(1)
    U_(0, 0)
    P_(1, 0, 1)
    ag(1, 1, 1)
    S_(1, 0)
    P_(1, 1, 1)
    U_(0, 1)
    transpose(w1T, w1)
    ag(1, 2, 0)
    U_(0, 3)
    V_(0, 2)
    S_(1, 1)
    ag(1, 2, 1)
    P_(1, 2, 1)
    S_(1, 2)
    V_(0, 1)
    transpose(upT, upb)
    V_(0, 3)
    GV(0, 2)
    V_(0, 0)
    U_(1, 0)
    ag(1, 3, 0)
    ag(1, 3, 1)
    P_(1, 3, 1)
    S_(1, 3)
    U_(1, 2)
    GV(0, 3)
    GV(0, 0)
    GU(0, 2)
    U_(1, 1)
    V_(1, 0)
    U_(1, 3)
    GV(0, 1)
    grad_mm(0, 2, 1)
    V_(1, 2)
    GU(0, 3)
    grad_mm(0, 3, 1)
    RS(0, 0)
    V_(1, 1)
    V_(1, 3)
    GU(0, 1)
    transpose(tokT, tokb)
    GV(1, 0)
    GV(1, 2)
    RS(0, 1)
    GU(0, 0)
    GV(1, 1)
    grad_mm(0, 1, 1)
    GV(1, 3)
    drain(40)
    RS(0, 2)
    GU(1, 2)
    GU(1, 1)
    GU(1, 0)
    grad_mm(1, 2, 1)
    GU(1, 3)
    grad_mm(1, 3, 1)
    RS(1, 0)
    grad_mm(1, 0, 2)
    TG()
    RS(1, 1)
    grad_mm(0, 0, 1)
    RS(0, 3)
    TG2()
    drain(40)
    RS(1, 2)
    drain(40)
    RS(1, 3)
    RS_end(0)
    TGE()
    RS_end(1)
    drain()
    for n in range(3):
        a2a_wait(n, a2a_send)


def finish(tg, ing, outg, tg_o, ing_o, outg_o, tf, sem):
    NC = 4
    D = tg.shape[1]
    C = D // NC
    c_o = pltpu.make_async_copy(outg, outg_o, sem.at[0])
    c_o.start()
    c_i = pltpu.make_async_copy(ing, ing_o, sem.at[1])
    c_i.start()
    outs = []
    for n in range(NC):
        cols = pl.ds(C * n, C)
        tf[:, cols] = tg[:, cols].astype(F32)
        o = pltpu.make_async_copy(tf.at[:, cols], tg_o.at[:, cols], sem.at[2 + NC + n])
        o.start()
        outs.append(o)
    c_o.wait()
    c_i.wait()
    for o in outs:
        o.wait()


def make(mesh):
    NXL, NDP, NZ = mesh.shape["dcn"], mesh.shape["dp"], mesh.shape["tp"]
    NP = NXL * NDP
    NS = 1
    while NS * NS * 2 < NP:
        NS += 1

    def per_device(tokens, upstream, w_in, w_out):
        T, D = tokens.shape
        B = D // NP
        BC = 2 * B
        H = NZ // 2
        HL = 128 * H
        R = NP * T
        RC = R // 2
        UR = R // NS
        VR = UR // NS
        cfg = (NXL, NDP, NZ, NS, T, B)
        DMA = pltpu.SemaphoreType.DMA
        VM = pltpu.VMEM
        scratch = [
            VM((R, BC), BF16),
            VM((R, BC), BF16),
            VM((BC, R), BF16),
            VM((BC, R), BF16),
            VM((BC, 128), BF16),
            VM((BC, 128), BF16),
            VM((BC, HL), BF16),
            VM((BC, HL), BF16),
            VM((HL, BC), BF16),
            VM((128, BC), BF16),
            VM((2, R, HL), F32),
            VM((2, NS - 1, UR, HL), F32),
            VM((2, UR, HL), F32),
            VM((2, NS - 1, VR, HL), F32),
            VM((2, NS, UR, 128), F32),
            VM((VR, HL), F32),
            VM((UR, 128), F32),
            VM((2, R, HL), BF16),
            VM((2, BC, HL), F32),
            VM((2, B, 128), F32),
            VM((2 * H, BC, 128), BF16),
            VM((2 * H, BC, 128), BF16),
            VM((2, 2, B, 128), BF16),
            VM((R, BC), F32),
            VM((RC, BC), F32),
            VM((RC, BC), BF16),
            DMA((5,)),
            DMA((3,)),
            DMA((3,)),
            DMA((5,)),
            DMA((5,)),
            DMA((8 * H,)),
            DMA((8 * H,)),
            DMA((8 * H,)),
            DMA((8 * H,)),
            DMA((8,)),
            DMA((4 * H, NS - 1)),
            DMA((4 * H, NS - 1)),
            DMA((4 * H, NS - 1)),
            DMA((4 * H, NS - 1)),
        ]
        tg, ing, outg = pl.pallas_call(
            functools.partial(kernel, cfg),
            out_shape=(
                jax.ShapeDtypeStruct((T, D), BF16),
                jax.ShapeDtypeStruct((B, 128), F32),
                jax.ShapeDtypeStruct((B, 128), F32),
            ),
            in_specs=[pl.BlockSpec(memory_space=pl.ANY)] * 4,
            out_specs=(
                pl.BlockSpec(memory_space=pl.ANY),
                pl.BlockSpec(memory_space=pltpu.VMEM),
                pl.BlockSpec(memory_space=pltpu.VMEM),
            ),
            scratch_shapes=scratch,
            compiler_params=pltpu.CompilerParams(
                collective_id=0, has_side_effects=True, vmem_limit_bytes=105 * 2**19
            ),
        )(tokens, upstream, w_in, w_out)
        tg_f, ing_f, outg_f = pl.pallas_call(
            finish,
            out_shape=(
                jax.ShapeDtypeStruct((T, D), F32),
                jax.ShapeDtypeStruct((B, 128), F32),
                jax.ShapeDtypeStruct((B, 128), F32),
            ),
            in_specs=[pl.BlockSpec(memory_space=pltpu.VMEM)] * 3,
            out_specs=tuple([pl.BlockSpec(memory_space=pl.ANY)] * 3),
            scratch_shapes=[
                pltpu.VMEM((T, D), F32),
                DMA((10,)),
            ],
            compiler_params=pltpu.CompilerParams(vmem_limit_bytes=50 * 2**20),
        )(tg, ing, outg)
        return tg_f, ing_f, outg_f.T

    return per_device


def solution(mesh):
    placed = (
        P(("dcn", "dp", "tp"), None),
        P(("dcn", "dp", "tp"), None),
        P(None, "tp"),
        P("tp", None),
    )
    return jax.shard_map(
        make(mesh),
        mesh=mesh,
        in_specs=placed,
        out_specs=(P(("dcn", "dp", "tp"), None), P(("dcn", "dp"), "tp"), P("tp", ("dcn", "dp"))),
        check_vma=False,
    )
```

```python
import functools

import jax
import jax.numpy as jnp
from jax import lax
from jax.experimental import pallas as pl
from jax.experimental.pallas import tpu as pltpu
from jax.sharding import PartitionSpec as P

MESH = pl.DeviceIdType.MESH
F32 = jnp.float32
BF16 = jnp.bfloat16


def mult(value, of):
    return pl.multiple_of(value, of)


def kernel(
    cfg,
    tokens, upstream, w_in, w_out,
    tg_out, ing_out, outg_out,
    tokb, upb, tokT, upT, own1, own2, w1, w2, w1T, wo_tmp,
    prep, urecv, usum, vrecv, vv, pos, posv, gath,
    grad, ownp, zsend, zrecv, zfin, tgp, tgx, tgb,
    loc_sem, a2a_send, a2a_recv, f_send, f_recv, ag_sent, ag_recv, rs_sent, rs_recv,
    fin_recv, u_send, u_recv, v_send, v_recv,
):
    NXL, NDP, NZ, NS, T, B = cfg
    NP = NXL * NDP
    NC = NP // 2
    H = NZ // 2
    BC = 2 * B
    R = NP * T
    RC = R // 2
    UR = R // NS
    VR = UR // NS
    HP = B // 2

    z = lax.axis_index("tp")
    dcn = lax.axis_index("dcn")
    dp = lax.axis_index("dp")
    k = dp % 2
    y = (dp // 2) % NS
    x = (dp // (2 * NS)) * NXL + dcn
    p = (dcn * NDP + dp) // 2
    u = jnp.where(k == 0, x, y)
    v = jnp.where(k == 0, y, x)
    up = (z + 1) % NZ
    down = (z + NZ - 1) % NZ

    def dev(x_, y_, k_):
        return (x_ % NXL, (x_ // NXL) * (2 * NS) + y_ * 2 + k_, z)

    def chip(p_):
        i_ = 2 * p_ + k
        return (i_ // NDP, i_ % NDP, z)

    def at_z(z_, k_):
        return (dcn, dp - k + k_, z_)

    sib = dev(x, y, 1 - k)

    def u_peer(u_):
        return dev(jnp.where(k == 0, u_, x), jnp.where(k == 0, y, u_), k)

    def v_peer(v_):
        return dev(jnp.where(k == 0, x, v_), jnp.where(k == 0, v_, y), k)

    ag_z = jnp.where(k == 0, up, down)
    rs_z = jnp.where(k == 0, down, up)

    sends = []

    def send(src, dst, ss, rs, to, when=None):
        c = pltpu.make_async_remote_copy(
            src_ref=src, dst_ref=dst, send_sem=ss, recv_sem=rs, device_id=to, device_id_type=MESH
        )
        if when is None:
            c.start()
        else:
            pl.when(when)(c.start)
        sends.append((when, c))
        return c

    def landed(ref, sem):
        pltpu.make_async_copy(ref, ref, sem).wait()

    def drain(keep=0):
        while len(sends) > keep:
            when, c = sends.pop(0)
            if when is None:
                c.wait_send()
            else:
                pl.when(when)(c.wait_send)

    LAST = H - 1

    def lanes(c, n=1):
        return pl.ds(128 * c, 128 * n)

    barrier = pltpu.get_barrier_semaphore()
    cols = pl.ds(mult(BC * p, 128), BC)
    my_tok = pl.ds(mult(RC * k + T * p, T), T)
    my_half = pl.ds(mult(RC * k, RC), RC)
    sib_half = pl.ds(mult(RC * (1 - k), RC), RC)

    def entry():
        for z_ in (up, down) if NZ > 2 else (up,):
            for k_ in (0, 1):
                pl.semaphore_signal(barrier, inc=1, device_id=at_z(z_, k_), device_id_type=MESH)
        pl.semaphore_signal(barrier, inc=1, device_id=sib, device_id_type=MESH)

        @pl.loop(1, NC)
        def _(d):
            pl.semaphore_signal(barrier, inc=1, device_id=chip((p + d) % NC), device_id_type=MESH)

    c_win = pltpu.make_async_copy(w_in.at[pl.ds(mult(BC * p, 128), BC), :], own1, loc_sem.at[0])
    c_wout = pltpu.make_async_copy(w_out.at[:, cols], wo_tmp, loc_sem.at[1])
    c_tok = pltpu.make_async_copy(tokens.at[:, cols], tokb.at[my_tok, :], loc_sem.at[2])
    c_up = pltpu.make_async_copy(upstream.at[:, cols], upb.at[my_tok, :], loc_sem.at[3])

    def entry_wait():
        pl.semaphore_wait(barrier, NC + (4 if NZ > 2 else 2))

    def own_wout():
        c_win.wait()
        c_wout.wait()
        own2[...] = wo_tmp[...].T

        @pl.when(k == 0)
        def _():
            w1[:, lanes(LAST)] = own1[...]
            w2[:, lanes(LAST)] = own2[...]

    def rows_at(q):
        return pl.ds(HP * q, HP)

    def ag_block(wi, step):
        return (own1, own2)[wi] if step == 0 else (w1, w2)[wi].at[:, lanes(step - 1)]

    def ag_sem(wi, step, q):
        return (wi * H + step) * 4 + q

    def ag_send(wi, step, q):
        w = (w1, w2)[wi]
        n = ag_sem(wi, step, q)
        if wi == 0 and step == 0:
            src = w_in.at[pl.ds(mult(BC * p + HP * q, 32), HP), :]
        else:
            src = ag_block(wi, step).at[rows_at(q), :]
        if step < H - 1:
            send(src, w.at[rows_at(q), lanes(step)], ag_sent.at[n], ag_recv.at[n], at_z(ag_z, k))
        else:
            send(
                src, w.at[rows_at(q), lanes(LAST)], ag_sent.at[n], ag_recv.at[n], at_z(ag_z, 1),
                when=k == q // 2,
            )


    def ag_start(wi):
        for q in range(4):
            ag_send(wi, 0, q)

    def ag(wi, step, half):
        w = (w1, w2)[wi]
        for q in (2 * half, 2 * half + 1):
            arrived = w.at[rows_at(q), lanes(step)]
            if step < H - 1:
                landed(arrived, ag_recv.at[ag_sem(wi, step, q)])
                ag_send(wi, step + 1, q)
            else:
                pl.when(k == 1)(functools.partial(landed, arrived, ag_recv.at[ag_sem(wi, step, q)]))

    def a2a_start(src, dst, n):
        @pl.loop(1, NC)
        def _(d):
            to = (p + d) % NC
            pltpu.make_async_remote_copy(
                src_ref=src.at[:, pl.ds(mult(BC * to, 128), BC)],
                dst_ref=dst.at[my_tok, :],
                send_sem=a2a_send.at[n],
                recv_sem=a2a_recv.at[n],
                device_id=chip(to),
                device_id_type=MESH,
            ).start()

    def a2a_wait(n, sems):
        landed(tokb.at[pl.ds(0, RC - T), :], sems.at[n])

    def A2F(n):
        (c_tok, c_up)[n].wait()
        a2a_wait(n, a2a_recv)
        ref = (tokb, upb)[n].at[my_half, :]
        send(ref, ref, f_send.at[n], f_recv.at[n], sib)

    def A2W(n):
        landed((tokb, upb)[n].at[sib_half, :], f_recv.at[n])

    mine = pl.ds(mult(UR * u + VR * v, VR), VR)
    u_rows = pl.ds(mult(UR * u, UR), UR)
    pend = {}

    def P_(n, c, count):
        lhs, w = ((tokb, w1), (upb, w2))[n]
        prep[n, :, lanes(c, count)] = jnp.dot(lhs[...], w[:, lanes(c, count)], preferred_element_type=F32)

    def S_(n, c):
        q = n * H + c
        out = []
        for r in [2, 1, 3] if NS == 4 else range(1, NS):
            uu = (u + r) % NS
            out.append(
                send(
                    prep.at[n, pl.ds(mult(UR * uu, UR), UR), lanes(c)], urecv.at[n, r - 1, :, lanes(c)],
                    u_send.at[q, r - 1], u_recv.at[q, r - 1], u_peer(uu),
                )
            )
        pend["u", n, c] = out

    def U_(n, c):
        q = n * H + c
        for d in pend["u", n, c]:
            d.wait_recv()
        tot = prep[n, u_rows, lanes(c)]
        for r in range(NS - 1):
            tot = tot + urecv[n, r, :, lanes(c)]
        usum[n, :, lanes(c)] = tot
        if c == -1:
            vv[n, v] = tot
            mine_all = usum.at[n, :, lanes(c)]
            pend["v", n, c] = [
                send(mine_all, vv.at[n, v], v_send.at[q, r - 1], v_recv.at[q, r - 1], v_peer((v + r) % NS))
                for r in range(1, NS)
            ]
            return
        pend["v", n, c] = [
            send(
                usum.at[n, pl.ds(mult(VR * ((v + r) % NS), VR), VR), lanes(c)], vrecv.at[n, r - 1, :, lanes(c)],
                v_send.at[q, r - 1], v_recv.at[q, r - 1], v_peer((v + r) % NS),
            )
            for r in range(1, NS)
        ]

    def V_(n, c):
        q = 2 * H + n * H + c
        for d in pend["v", n, c]:
            d.wait_recv()
        if c == -1:
            tot = vv[n, 0]
            for r in range(1, NS):
                tot = tot + vv[n, r]
            if n == 0:
                positive = jnp.maximum(tot, 0.0)
                posv[...] = positive
                gath[0, u_rows, lanes(c)] = (positive * positive).astype(BF16)
            else:
                gath[1, u_rows, lanes(c)] = (tot * 2.0 * posv[...]).astype(BF16)
            return
        tot = usum[n, pl.ds(mult(VR * v, VR), VR), lanes(c)]
        for r in range(NS - 1):
            tot = tot + vrecv[n, r, :, lanes(c)]
        if n == 0:
            positive = jnp.maximum(tot, 0.0)
            pos[:, lanes(c)] = positive
            gath[0, mine, lanes(c)] = (positive * positive).astype(BF16)
        else:
            gath[1, mine, lanes(c)] = (tot * 2.0 * pos[:, lanes(c)]).astype(BF16)
        ref = gath.at[n, mine, lanes(c)]
        pend["gv", n, c] = [
            send(ref, ref, v_send.at[q, r - 1], v_recv.at[q, r - 1], v_peer((v + r) % NS)) for r in range(1, NS)
        ]

    def GV(n, c):
        q = 2 * H + n * H + c
        if c != -1:
            for d in pend["gv", n, c]:
                d.wait_recv()
        ref = gath.at[n, u_rows, lanes(c)]
        pend["gu", n, c] = [
            send(ref, ref, u_send.at[q, r - 1], u_recv.at[q, r - 1], u_peer((u + r) % NS)) for r in range(1, NS)
        ]

    def GU(n, c):
        for d in pend["gu", n, c]:
            d.wait_recv()

    def grad_mm(n, c, count):
        lhsT = (upT, tokT)[n]
        grad[n, :, lanes(c, count)] = jnp.dot(lhsT[...], gath[n, :, lanes(c, count)], preferred_element_type=F32)

    def half_rows(hf):
        return pl.ds(mult(B * hf, 64), B)

    def rs_one(n, step, hf, recv):
        q = n * H + step
        for m in (0, 1):
            rows = pl.ds(mult(B * hf + HP * m, 32), HP)
            val = grad[n, rows, lanes(H - 1 - step)]
            if recv:
                landed(zrecv.at[q - 1, rows, :], rs_recv.at[4 * (q - 1) + 2 * hf + m])
                val = val + zrecv[q - 1, rows, :].astype(F32)
            zsend[q, rows, :] = val.astype(BF16)
            src = zsend.at[q, rows, :]
            s = 4 * q + 2 * hf + m
            if step < H - 1:
                send(src, zrecv.at[q, rows, :], rs_sent.at[s], rs_recv.at[s], at_z(rs_z, k))
            else:
                dst = zfin.at[n, k, pl.ds(HP * m, HP), :]
                send(src, dst, rs_sent.at[s], fin_recv.at[4 * n + 2 * k + m], at_z(rs_z, hf))

    def RS(n, step):
        if step == 0:
            q = n * H

            @pl.when(k == 1)
            def _():
                zsend[q] = grad[n, :, lanes(LAST)].astype(BF16)

            for hf, to in ((0, at_z(up, 1)), (1, at_z(down, 0))):
                for m in (0, 1):
                    rows = pl.ds(B * hf + HP * m, HP)
                    s = 4 * q + 2 * hf + m
                    send(
                        zsend.at[q, rows, :], zrecv.at[q, rows, :], rs_sent.at[s], rs_recv.at[s], to, when=k == 1
                    )
            rs_one(n, 1, k, False)
            send(
                grad.at[n, pl.ds(B, B), lanes(LAST)], ownp.at[n], f_send.at[2 + n], f_recv.at[2 + n], sib, when=k == 0
            )
        elif step == 1:
            rs_one(n, 1, 1 - k, True)
        else:
            rs_one(n, step, k, True)
            rs_one(n, step, 1 - k, True)

    def RS_end(n):
        for d in (0, 1):
            for m in (0, 1):
                landed(zfin.at[n, d, pl.ds(HP * m, HP), :], fin_recv.at[4 * n + 2 * d + m])
        tot = zfin[n, 0].astype(F32) + zfin[n, 1].astype(F32)

        @pl.when(k == 0)
        def _():
            (outg_out, ing_out)[n][...] = tot + grad[n, 0:B, lanes(LAST)]

        @pl.when(k == 1)
        def _():
            landed(ownp.at[n], f_recv.at[2 + n])
            (outg_out, ing_out)[n][...] = tot + ownp[n]

    TR = min(128, RC)

    def tg_mm(half):
        @pl.loop(0, RC // TR)
        def _(t):
            rows = pl.ds(mult(RC * half + TR * t, TR), TR)
            tgp[rows, :] = jnp.dot(gath[1, rows, :], w1T[...], preferred_element_type=F32)

    def TG():
        tg_mm(1 - k)
        send(tgp.at[sib_half, :], tgx, f_send.at[4], f_recv.at[4], sib)
        tg_mm(k)

    c_t = pltpu.make_async_copy(tgb.at[pl.ds(mult(T * p, T), T), :], tg_out.at[:, cols], loc_sem.at[4])

    def TG2():
        landed(tgx, f_recv.at[4])

        @pl.loop(0, RC // TR)
        def _(t):
            rows = pl.ds(mult(TR * t, TR), TR)
            tgb[rows, :] = (tgp[pl.ds(mult(RC * k + TR * t, TR), TR), :] + tgx[rows, :]).astype(BF16)

        @pl.loop(1, NC)
        def _(d):
            to = (p + d) % NC
            pltpu.make_async_remote_copy(
                src_ref=tgb.at[pl.ds(mult(T * to, T), T), :],
                dst_ref=tg_out.at[:, cols],
                send_sem=a2a_send.at[2],
                recv_sem=a2a_recv.at[2],
                device_id=chip(to),
                device_id_type=MESH,
            ).start()

        c_t.start()

    def TGE():
        landed(tg_out.at[:, pl.ds(0, BC * (NC - 1))], a2a_recv.at[2])
        c_t.wait()

    def transpose(dst, src):
        dst[...] = src[...].T

    entry()
    for c in (c_win, c_wout, c_tok, c_up):
        c.start()
    entry_wait()
    ag_start(0)
    a2a_start(tokens, tokb, 0)
    ag(0, 0, 0)
    ag(0, 0, 1)
    a2a_start(upstream, upb, 1)
    ag(0, 1, 0)
    own_wout()
    ag(0, 1, 1)
    A2F(0)
    ag_start(1)
    A2W(0)
    P_(0, 0, 1)
    S_(0, 0)
    ag(0, 2, 0)
    ag(0, 2, 1)
    P_(0, 2, 1)
    S_(0, 2)
    P_(0, 1, 1)
    S_(0, 1)
    ag(1, 0, 0)
    A2F(1)
    ag(1, 0, 1)
    ag(0, 3, 1)
    ag(0, 3, 0)
    P_(0, 3, 1)
    S_(0, 3)
    ag(1, 1, 0)
    U_(0, 2)
    A2W(1)
    U_(0, 0)
    P_(1, 0, 1)
    ag(1, 1, 1)
    S_(1, 0)
    P_(1, 1, 1)
    U_(0, 1)
    transpose(w1T, w1)
    ag(1, 2, 0)
    U_(0, 3)
    V_(0, 2)
    S_(1, 1)
    ag(1, 2, 1)
    P_(1, 2, 1)
    S_(1, 2)
    V_(0, 1)
    transpose(upT, upb)
    V_(0, 3)
    GV(0, 2)
    V_(0, 0)
    U_(1, 0)
    ag(1, 3, 0)
    ag(1, 3, 1)
    P_(1, 3, 1)
    S_(1, 3)
    U_(1, 2)
    GV(0, 3)
    GV(0, 0)
    GU(0, 2)
    U_(1, 1)
    V_(1, 0)
    U_(1, 3)
    GV(0, 1)
    grad_mm(0, 2, 1)
    V_(1, 2)
    GU(0, 3)
    grad_mm(0, 3, 1)
    RS(0, 0)
    V_(1, 1)
    V_(1, 3)
    GU(0, 1)
    transpose(tokT, tokb)
    GV(1, 0)
    GV(1, 2)
    RS(0, 1)
    GU(0, 0)
    GV(1, 1)
    grad_mm(0, 1, 1)
    GV(1, 3)
    drain(40)
    rs_one(0, 2, k, True)
    GU(1, 2)
    grad_mm(1, 2, 1)
    rs_one(0, 2, 1 - k, True)
    GU(1, 1)
    GU(1, 0)
    GU(1, 3)
    grad_mm(1, 3, 1)
    RS(1, 0)
    grad_mm(1, 0, 2)
    TG()
    RS(1, 1)
    grad_mm(0, 0, 1)
    RS(0, 3)
    TG2()
    drain(40)
    RS(1, 2)
    drain(40)
    RS(1, 3)
    RS_end(0)
    TGE()
    RS_end(1)
    drain()
    for n in range(3):
        a2a_wait(n, a2a_send)


def finish(tg, ing, outg, tg_o, ing_o, outg_o, tf, sem):
    NC = 4
    D = tg.shape[1]
    C = D // NC
    c_o = pltpu.make_async_copy(outg, outg_o, sem.at[0])
    c_o.start()
    c_i = pltpu.make_async_copy(ing, ing_o, sem.at[1])
    c_i.start()
    outs = []
    for n in range(NC):
        cols = pl.ds(C * n, C)
        tf[:, cols] = tg[:, cols].astype(F32)
        o = pltpu.make_async_copy(tf.at[:, cols], tg_o.at[:, cols], sem.at[2 + NC + n])
        o.start()
        outs.append(o)
    c_o.wait()
    c_i.wait()
    for o in outs:
        o.wait()


def make(mesh):
    NXL, NDP, NZ = mesh.shape["dcn"], mesh.shape["dp"], mesh.shape["tp"]
    NP = NXL * NDP
    NS = 1
    while NS * NS * 2 < NP:
        NS += 1

    def per_device(tokens, upstream, w_in, w_out):
        T, D = tokens.shape
        B = D // NP
        BC = 2 * B
        H = NZ // 2
        HL = 128 * H
        R = NP * T
        RC = R // 2
        UR = R // NS
        VR = UR // NS
        cfg = (NXL, NDP, NZ, NS, T, B)
        DMA = pltpu.SemaphoreType.DMA
        VM = pltpu.VMEM
        scratch = [
            VM((R, BC), BF16),
            VM((R, BC), BF16),
            VM((BC, R), BF16),
            VM((BC, R), BF16),
            VM((BC, 128), BF16),
            VM((BC, 128), BF16),
            VM((BC, HL), BF16),
            VM((BC, HL), BF16),
            VM((HL, BC), BF16),
            VM((128, BC), BF16),
            VM((2, R, HL), F32),
            VM((2, NS - 1, UR, HL), F32),
            VM((2, UR, HL), F32),
            VM((2, NS - 1, VR, HL), F32),
            VM((2, NS, UR, 128), F32),
            VM((VR, HL), F32),
            VM((UR, 128), F32),
            VM((2, R, HL), BF16),
            VM((2, BC, HL), F32),
            VM((2, B, 128), F32),
            VM((2 * H, BC, 128), BF16),
            VM((2 * H, BC, 128), BF16),
            VM((2, 2, B, 128), BF16),
            VM((R, BC), F32),
            VM((RC, BC), F32),
            VM((RC, BC), BF16),
            DMA((5,)),
            DMA((3,)),
            DMA((3,)),
            DMA((5,)),
            DMA((5,)),
            DMA((8 * H,)),
            DMA((8 * H,)),
            DMA((8 * H,)),
            DMA((8 * H,)),
            DMA((8,)),
            DMA((4 * H, NS - 1)),
            DMA((4 * H, NS - 1)),
            DMA((4 * H, NS - 1)),
            DMA((4 * H, NS - 1)),
        ]
        tg, ing, outg = pl.pallas_call(
            functools.partial(kernel, cfg),
            out_shape=(
                jax.ShapeDtypeStruct((T, D), BF16),
                jax.ShapeDtypeStruct((B, 128), F32),
                jax.ShapeDtypeStruct((B, 128), F32),
            ),
            in_specs=[pl.BlockSpec(memory_space=pl.ANY)] * 4,
            out_specs=(
                pl.BlockSpec(memory_space=pl.ANY),
                pl.BlockSpec(memory_space=pltpu.VMEM),
                pl.BlockSpec(memory_space=pltpu.VMEM),
            ),
            scratch_shapes=scratch,
            compiler_params=pltpu.CompilerParams(
                collective_id=0, has_side_effects=True, vmem_limit_bytes=105 * 2**19
            ),
        )(tokens, upstream, w_in, w_out)
        tg_f, ing_f, outg_f = pl.pallas_call(
            finish,
            out_shape=(
                jax.ShapeDtypeStruct((T, D), F32),
                jax.ShapeDtypeStruct((B, 128), F32),
                jax.ShapeDtypeStruct((B, 128), F32),
            ),
            in_specs=[pl.BlockSpec(memory_space=pltpu.VMEM)] * 3,
            out_specs=tuple([pl.BlockSpec(memory_space=pl.ANY)] * 3),
            scratch_shapes=[
                pltpu.VMEM((T, D), F32),
                DMA((10,)),
            ],
            compiler_params=pltpu.CompilerParams(vmem_limit_bytes=50 * 2**20),
        )(tg, ing, outg)
        return tg_f, ing_f, outg_f.T

    return per_device


def solution(mesh):
    placed = (
        P(("dcn", "dp", "tp"), None),
        P(("dcn", "dp", "tp"), None),
        P(None, "tp"),
        P("tp", None),
    )
    return jax.shard_map(
        make(mesh),
        mesh=mesh,
        in_specs=placed,
        out_specs=(P(("dcn", "dp", "tp"), None), P(("dcn", "dp"), "tp"), P("tp", ("dcn", "dp"))),
        check_vma=False,
    )
```
